512 devices in a mesh: gx: 32 (over z, core), gy: 8 (over y, x_lo), gz: 2 (over x_hi).
Axes of the slice: x: 4 (x_hi: 2, x_lo: 2; x = x_hi * 2 + x_lo), y: 4, z: 16, core: 2. Of those that a mesh axis runs over, the one named last changes fastest.
Arguments:
- adjoint: float32 [2, 4, 16, 256, 1024], P(None, None, 'gz', 'gx', 'gy'), may hold values from -6 to 6
- saved_state: float32 [4, 4, 16, 256, 1024], P(None, None, 'gz', 'gx', 'gy'), may hold values from -6 to 6
- wind_field: float32 [3, 16, 256, 1024], P(None, 'gz', 'gx', 'gy'), may hold values from -0.3 to 0.3
- facade_slot: int32 [16, 256, 1024], P('gz', 'gx', 'gy'), may hold values from 0 to 64, as said below
- facade_table: int32 [2, 32, 8, 64], P('gz', 'gx', 'gy'), may hold values from 0 to 16383, as said below
- impedance: float32 [16384], replicated, may hold values from 0.1 to 1
Outputs:
- adjoint_out: float32 [2, 4, 16, 256, 1024], P(None, None, 'gz', 'gx', 'gy')
- gradient: float32 [16384], P(('gx', 'gy', 'gz'))
The draws below stay inside these ranges and needn't reach their ends.
Inputs may be any that keep to these rules, and one draw needn't show every extreme that they name: `facade_slot`: slots name entries of the cell's own device block table. `facade_table`: A block's facades are owned by that block's device or by one of the two devices beside it along gx (wrapping), the owner of facade f being the device of index f // 32 along gx+gy+gz; ids may repeat within and across tables.
All inputs are finite; a program needn't handle non-finite values.
Results may differ from the reference program's by a relative error of at most 0.00013.
Values sent between devices are 32-bit elements; how exact they have to be, the bound alone decides.
A program may use at most 64 MiB of HBM per device.

```python
import math
import jax
import jax.numpy as jnp

CX = 8
CY = 128
CZ = 8
STEPS = 4
LOC = 64
FAC_DEV = 32
NX = 256
NY = 1024
NZ = 16
FACADES = 16384


def draw_facade_slot(key, part):
    key_level, key_cell, key_slot = jax.random.split(key, 3)
    level = jax.random.randint(key_level, (NZ // CZ, NX // CX, NY // CY), 0, 4)
    density = jnp.left_shift(jnp.int32(1), level.astype(jnp.int32))
    cell_density = jnp.repeat(jnp.repeat(jnp.repeat(density, CZ, axis=0), CX, axis=1), CY, axis=2)
    on_facade = jax.random.randint(key_cell, (NZ, NX, NY), 0, 16) < cell_density
    slot_of = jax.random.randint(key_slot, (NZ, NX, NY), 1, LOC + 1)
    result = jnp.where(on_facade, slot_of, 0)
    result = result.at[0, 0, 0].set(LOC).at[0, 0, 1].set(0)
    return result.astype(jnp.int32)


def draw_facade_table(key, part):
    key_offset, key_name = jax.random.split(jax.random.fold_in(key, 7), 2)
    blocks_z = NZ // CZ
    blocks_x = NX // CX
    blocks_y = NY // CY
    shape = (blocks_z, blocks_x, blocks_y, LOC)
    offset = jax.random.randint(key_offset, shape, -1, 2)
    block_z = jnp.arange(blocks_z, dtype=jnp.int32)[:, None, None, None]
    block_x = jnp.arange(blocks_x, dtype=jnp.int32)[None, :, None, None]
    block_y = jnp.arange(blocks_y, dtype=jnp.int32)[None, None, :, None]
    owner_x = (block_x + offset + blocks_x) % blocks_x
    owner_block = (owner_x * blocks_y + block_y) * blocks_z + block_z
    result = owner_block * FAC_DEV + jax.random.randint(key_name, shape, 0, FAC_DEV)
    total = FAC_DEV * blocks_z * blocks_x * blocks_y
    result = result.at[0, 0, 0, 0].set(0).at[blocks_z - 1, blocks_x - 1, blocks_y - 1, LOC - 1].set(total - 1)
    return result.astype(jnp.int32)


def levels(rng, extent, cuts, least, largest):
    def one(dim, shards_of):
        heights = jax.random.uniform(jax.random.fold_in(jax.random.fold_in(rng, 6), dim), (shards_of,), jnp.float32, least / len(cuts), largest / len(cuts))
        return jnp.repeat(jnp.exp(heights), extent[dim] // shards_of).reshape((-1,) + (1,) * (len(extent) - dim - 1))

    gain = one(*cuts[0])
    for cut in cuts[1:]:
        gain = gain * one(*cut)
    return gain


def normal_values(key, extent, scale, most, cuts=(), kind=jnp.bfloat16):
    array = jax.random.normal(key, extent, jnp.float32) * scale
    if len(cuts) > 0:
        array = levels(key, extent, cuts, -0.22, 0.18) * array
    return jnp.clip(array, min=-most, max=most).astype(kind)


def setup_inputs(seed: int = 0) -> dict:
    streams_of = jax.random.split(jax.random.key(seed), 7)
    return {
        "adjoint": normal_values(streams_of[0], (2, 4, NZ, NX, NY), 1.0, 6.0, ((2, 2), (3, 32), (4, 8)), jnp.float32),
        "saved_state": normal_values(streams_of[1], (STEPS, 4, NZ, NX, NY), 1.0, 6.0, ((2, 2), (3, 32), (4, 8)), jnp.float32),
        "wind_field": jnp.clip(jax.random.uniform(streams_of[2], (3, NZ, NX, NY), jnp.float32, -0.3, 0.3) * levels(streams_of[2], (3, NZ, NX, NY), ((1, 2), (2, 32), (3, 8)), -0.4, 0.0), -0.3, 0.3),
        "facade_slot": draw_facade_slot(jax.random.fold_in(streams_of[6], 71), 0),
        "facade_table": draw_facade_table(jax.random.fold_in(streams_of[6], 71), 0),
        "impedance": jnp.clip(jnp.exp(jax.random.uniform(streams_of[5], (FACADES,), jnp.float32, math.log(0.1), math.log(1.0))), 0.1, 1.0),
    }


TIME_STEP = 0.3


def trimmed(field, axis_k, offset):
    selector = [slice(None)] * field.ndim
    for j in range(3):
        dim = field.ndim - 3 + j
        length = field.shape[dim]
        if j == axis_k:
            selector[dim] = slice(1 + offset, length - 1 + offset)
        else:
            selector[dim] = slice(1, length - 1)
    return field[tuple(selector)]


def interior(field):
    return trimmed(field, 0, 0)


def central_diff(field, axis_k):
    return 0.5 * (trimmed(field, axis_k, 1) - trimmed(field, axis_k, -1))


def tendency(state_pad, wind_pad, damping_pad):
    pressure = state_pad[0]
    damping = interior(damping_pad)
    result = []
    for index in range(4):
        component = state_pad[index]
        advection = central_diff(wind_pad[0] * component, 0) + central_diff(wind_pad[1] * component, 1) + central_diff(wind_pad[2] * component, 2)
        if index == 0:
            coupling = central_diff(state_pad[1], 0) + central_diff(state_pad[2], 1) + central_diff(state_pad[3], 2)
        else:
            coupling = central_diff(pressure, index - 1)
        result.append(advection + coupling - damping * interior(component))
    return jnp.stack(result)


def padded_one(field):
    return jnp.pad(field, [(0, 0)] * (field.ndim - 3) + [(1, 1)] * 3)


def reference(adjoint, saved_state, wind_field, facade_slot, facade_table, impedance):
    blocks_x = NX // CX
    blocks_y = NY // CY
    block_z = (jnp.arange(NZ, dtype=jnp.int32) // CZ)[:, None, None]
    block_x = (jnp.arange(NX, dtype=jnp.int32) // CX)[None, :, None]
    block_y = (jnp.arange(NY, dtype=jnp.int32) // CY)[None, None, :]
    on_facade = facade_slot > 0
    flat_index = ((block_z * blocks_x + block_x) * blocks_y + block_y) * LOC + jnp.maximum(facade_slot - 1, 0)
    facade_of = facade_table.reshape(-1)[flat_index.astype(jnp.int32)]
    damping = jnp.where(on_facade, impedance[facade_of], jnp.float32(0.0))
    wind_pad = padded_one(wind_field)
    damping_pad = padded_one(damping)
    upper = adjoint[0]
    middle = adjoint[1]
    products = jnp.zeros((NZ, NX, NY), jnp.float32)
    for step in range(STEPS):
        products = products + jnp.sum(middle * saved_state[step], axis=0)
        newest = upper + 2.0 * TIME_STEP * tendency(padded_one(middle), wind_pad, damping_pad)
        upper, middle = middle, newest
    terms = jnp.where(on_facade, -2.0 * TIME_STEP * products, jnp.float32(0.0)).reshape(-1)
    owners = jnp.where(on_facade, facade_of, 0).reshape(-1).astype(jnp.int32)
    gradient = jax.ops.segment_sum(terms, owners, num_segments=FACADES)
    return jnp.stack([upper, middle]), gradient
```

```python
import functools

import jax
import jax.numpy as jnp
from jax import lax
from jax.experimental import pallas as pl
from jax.experimental.pallas import tpu as pltpu
from jax.sharding import PartitionSpec as P

FAC_DEV = 32
TIME_STEP = 0.3
HALF = TIME_STEP
FULL = 2.0 * TIME_STEP
MESH = pl.DeviceIdType.MESH
F32 = jnp.float32


def kernel(sizes, steps, adj, saved, wind, slot, table, imp, out, grad,
           mid, upp, sav, win, slo, tab, damp, part, prod, flux_z,
           xs, ys, zs, xr, yr, zr, smat, gs, gr,
           in_sem, x_ss, x_rs, y_ss, y_rs, z_ss, z_rs, g_ss, g_rs):
    nx, ny, nz = sizes
    ix, iy, iz = lax.axis_index("gx"), lax.axis_index("gy"), lax.axis_index("gz")
    right = (lax.rem(ix + 1, nx), iy, iz)
    left = (lax.rem(ix + nx - 1, nx), iy, iz)
    north = (ix, lax.rem(iy + 1, ny), iz)
    south = (ix, lax.rem(iy + ny - 1, ny), iz)
    other = (ix, iy, 1 - iz)
    barrier = pltpu.get_barrier_semaphore()
    for dev in (left, right, south, north, other):
        pl.semaphore_signal(barrier, inc=1, device_id=dev, device_id_type=MESH)

    loads = []
    for i, (src, dst) in enumerate(
        [(wind, win), (adj.at[1], mid), (table, tab), (slot, slo), (adj.at[0], upp), (saved, sav)]
    ):
        copy = pltpu.make_async_copy(src, dst, in_sem.at[i])
        copy.start()
        loads.append(copy)

    lane = lax.broadcasted_iota(jnp.int32, (8, 128), 1)
    row = lax.broadcasted_iota(jnp.int32, (8, 128), 0)
    first_row, last_row = row == 0, row == 7
    first_lane, last_lane = lane == 0, lane == 127
    odd = lax.rem(lane, 2) == 1

    def fluxes(c, s, w0, w1, w2):
        own = s[c]
        fz, fx, fy = w0 * own, w1 * own, w2 * own
        if c == 0:
            fz, fx, fy = fz + s[1], fx + s[2], fy + s[3]
        elif c == 1:
            fz = fz + s[0]
        elif c == 2:
            fx = fx + s[0]
        else:
            fy = fy + s[0]
        return fz, fx, fy

    def faces(k, m):
        low = jnp.zeros((8, 128), F32)
        high = jnp.zeros((8, 128), F32)
        allf = [[None] * 8 for _ in range(4)]
        for z in range(8):
            w0, w1, w2 = win[0, z], win[1, z], win[2, z]
            s = [m[c][z] for c in range(4)]
            for c in range(4):
                fz, fx, fy = fluxes(c, s, w0, w1, w2)
                allf[c][z] = (fz, fx, fy)
                n = c * 8 + z
                xs[k, 0, pl.ds(n, 1), :] = fx[0:1]
                xs[k, 1, pl.ds(n, 1), :] = fx[7:8]
                p = 2 * n + 1
                moved = pltpu.roll(fy, p + 1, 1)
                high = jnp.where(lane == p, moved, high)
                low = jnp.where(lane == p + 1, moved, low)
        ys[k, 0] = low
        ys[k, 1] = high
        for c in range(4):
            zs[k, c] = jnp.where(iz == 0, allf[c][7][0], allf[c][0][0])
        return allf

    def copies(k):
        mk = pltpu.make_async_remote_copy
        return [
            mk(src_ref=ys.at[k, 1], dst_ref=yr.at[k, 0], send_sem=y_ss.at[k, 0], recv_sem=y_rs.at[k, 0], device_id=north, device_id_type=MESH),
            mk(src_ref=ys.at[k, 0], dst_ref=yr.at[k, 1], send_sem=y_ss.at[k, 1], recv_sem=y_rs.at[k, 1], device_id=south, device_id_type=MESH),
            mk(src_ref=zs.at[k], dst_ref=zr.at[k], send_sem=z_ss.at[k], recv_sem=z_rs.at[k], device_id=other, device_id_type=MESH),
            mk(src_ref=xs.at[k, 1], dst_ref=xr.at[k, 0], send_sem=x_ss.at[k, 0], recv_sem=x_rs.at[k, 0], device_id=right, device_id_type=MESH),
            mk(src_ref=xs.at[k, 0], dst_ref=xr.at[k, 1], send_sem=x_ss.at[k, 1], recv_sem=x_rs.at[k, 1], device_id=left, device_id_type=MESH),
        ]

    def inner(m, allf, upper):
        for z in range(8):
            d = damp[z] * FULL
            for c in range(4):
                fz, fx, fy = allf[c][z]
                dx = jnp.where(last_row, 0.0, pltpu.roll(fx, 7, 0)) - jnp.where(first_row, 0.0, pltpu.roll(fx, 1, 0))
                dy = jnp.where(last_lane, 0.0, pltpu.roll(fy, 127, 1)) - jnp.where(first_lane, 0.0, pltpu.roll(fy, 1, 1))
                total = dx + dy
                if z < 7:
                    total = total + allf[c][z + 1][0]
                if z > 0:
                    total = total - allf[c][z - 1][0]
                part[c, z] = upper[c][z] + HALF * total - d * m[c][z]

    def finish(k):
        low = jnp.where(iy > 0, -yr[k, 0], 0.0)
        high = jnp.where(iy < ny - 1, pltpu.roll(yr[k, 1], 126, 1), 0.0)
        both = HALF * jnp.where(odd, low, high)
        from_left = jnp.where(ix > 0, -HALF, 0.0)
        from_right = jnp.where(ix < nx - 1, HALF, 0.0)
        top = jnp.where(iz == 0, HALF, 0.0)
        bottom = jnp.where(iz == 0, 0.0, HALF)
        m = [[None] * 8 for _ in range(4)]
        for z in range(8):
            for c in range(4):
                n = c * 8 + z
                value = part[c, z]
                edge = pltpu.roll(both, 128 - (2 * n + 1), 1)
                value = value + jnp.where(first_lane | last_lane, edge, 0.0)
                lrow = xr[k, 0, pl.ds(n, 1), :] * from_left
                rrow = xr[k, 1, pl.ds(n, 1), :] * from_right
                value = value + jnp.where(first_row, lrow, jnp.where(last_row, rrow, 0.0))
                if z == 7:
                    value = value + top * zr[k, c]
                if z == 0:
                    value = value - bottom * zr[k, c]
                m[c][z] = value
        return m

    def add_products(k, m):
        for z in range(8):
            total = m[0][z] * sav[k, 0, z]
            for c in range(1, 4):
                total = total + m[c][z] * sav[k, c, z]
            prod[z] = total if k == 0 else prod[z] + total

    loads[0].wait()
    loads[1].wait()
    m = [[mid[c, z] for z in range(8)] for c in range(4)]
    allf = faces(0, m)
    pl.semaphore_wait(barrier, 5)
    sends = copies(0)
    for copy in sends:
        copy.start()
    everything = list(sends)

    loads[2].wait()
    loads[3].wait()
    group = iy * nz + iz
    per_row = 128 // FAC_DEV
    stride = (ny * nz) // per_row
    row_of = [lax.rem(ix + o + nx, nx) * stride + group // per_row for o in (0, 1, -1)]
    ids = jnp.broadcast_to(tab[...], (8, 128))
    id_row = lax.shift_right_logical(ids, 7)
    id_lane = jnp.bitwise_and(ids, 127)
    lut = jnp.zeros((8, 128), F32)
    for o in range(3):
        line = jnp.broadcast_to(imp[pl.ds(row_of[o], 1), :], (8, 128))
        lut = jnp.where(id_row == row_of[o], jnp.take_along_axis(line, id_lane, axis=1), lut)
    place = jnp.where(id_row == row_of[0], 0, jnp.where(id_row == row_of[1], 32, 64)) + jnp.bitwise_and(ids, 31)
    for z in range(8):
        names = slo[z]
        value = jnp.take_along_axis(lut, jnp.maximum(names - 1, 0), axis=1)
        damp[z] = jnp.where(names > 0, value, 0.0)

    loads[4].wait()
    inner(m, allf, [[upp[c, z] for z in range(8)] for c in range(4)])
    loads[5].wait()
    add_products(0, m)

    older = m
    for k in range(steps):
        for copy in sends:
            copy.wait_recv()
        new = finish(k)
        if k == steps - 1:
            for c in range(4):
                for z in range(8):
                    out[1, c, z] = new[c][z]
            break
        for c in range(4):
            for z in range(8):
                if k == steps - 2:
                    out[0, c, z] = new[c][z]
        allf = faces(k + 1, new)
        sends = copies(k + 1)
        for copy in sends:
            copy.start()
        everything += sends
        add_products(k + 1, new)
        if k == steps - 2:
            for s in range(64):
                total = jnp.zeros((8, 128), F32)
                for z in range(8):
                    total = total + jnp.where(slo[z] == s + 1, prod[z], 0.0)
                smat[pl.ds(s, 1), :] = jnp.sum(total, axis=0, keepdims=True)
            sums = jnp.sum(smat[...], axis=1, keepdims=True) * (-FULL)
            turned = jnp.transpose(jnp.broadcast_to(place[0:1], (128, 128)))[0:64]
            wide = lax.broadcasted_iota(jnp.int32, (64, 128), 1)
            facades = jnp.sum(jnp.where(turned == wide, sums, 0.0), axis=0, keepdims=True)
            gs[...] = jnp.broadcast_to(facades, (8, 128))
            g_sends = [
                pltpu.make_async_remote_copy(src_ref=gs, dst_ref=gr.at[0], send_sem=g_ss.at[0], recv_sem=g_rs.at[0], device_id=right, device_id_type=MESH),
                pltpu.make_async_remote_copy(src_ref=gs, dst_ref=gr.at[1], send_sem=g_ss.at[1], recv_sem=g_rs.at[1], device_id=left, device_id_type=MESH),
            ]
            for copy in g_sends:
                copy.start()
        inner(new, allf, older)
        older = new
    for copy in g_sends:
        copy.wait_recv()
    total = gs[...] + pltpu.roll(gr[0], 96, 1) + pltpu.roll(gr[1], 64, 1)
    grad[...] = total[0:1]
    for copy in everything + g_sends:
        copy.wait_send()


def local(sizes, adjoint, saved_state, wind_field, facade_slot, facade_table, impedance):
    steps = saved_state.shape[0]
    table = jnp.pad(facade_table.reshape(1, -1), ((0, 0), (0, 64)))
    imp = impedance.reshape(-1, 128)
    any_spec = pl.BlockSpec(memory_space=pl.ANY)
    vmem_spec = pl.BlockSpec(memory_space=pltpu.VMEM)
    v = pltpu.VMEM
    dma = pltpu.SemaphoreType.DMA
    out, grad = pl.pallas_call(
        functools.partial(kernel, sizes, steps),
        out_shape=[
            jax.ShapeDtypeStruct(adjoint.shape, F32),
            jax.ShapeDtypeStruct((1, 128), F32),
        ],
        in_specs=[any_spec] * 5 + [vmem_spec],
        out_specs=[vmem_spec, vmem_spec],
        scratch_shapes=[
            v((4, 8, 8, 128), F32),
            v((4, 8, 8, 128), F32),
            v((steps, 4, 8, 8, 128), F32),
            v((3, 8, 8, 128), F32),
            v((8, 8, 128), jnp.int32),
            v((1, 128), jnp.int32),
            v((8, 8, 128), F32),
            v((4, 8, 8, 128), F32),
            v((8, 8, 128), F32),
            v((8, 128), F32),
            v((steps, 2, 32, 128), F32),
            v((steps, 2, 8, 128), F32),
            v((steps, 4, 8, 128), F32),
            v((steps, 2, 32, 128), F32),
            v((steps, 2, 8, 128), F32),
            v((steps, 4, 8, 128), F32),
            v((64, 128), F32),
            v((8, 128), F32),
            v((2, 8, 128), F32),
            dma((6,)),
            dma((steps, 2)), dma((steps, 2)), dma((steps, 2)), dma((steps, 2)),
            dma((steps,)), dma((steps,)), dma((2,)), dma((2,)),
        ],
        compiler_params=pltpu.CompilerParams(
            collective_id=0, has_side_effects=True, vmem_limit_bytes=32 << 20
        ),
    )(adjoint, saved_state, wind_field, facade_slot, table, imp)
    return out, grad[0, :FAC_DEV]


def solution(mesh):
    sizes = tuple(mesh.shape[a] for a in ("gx", "gy", "gz"))
    return jax.shard_map(
        functools.partial(local, sizes),
        mesh=mesh,
        in_specs=(
            P(None, None, "gz", "gx", "gy"),
            P(None, None, "gz", "gx", "gy"),
            P(None, "gz", "gx", "gy"),
            P("gz", "gx", "gy"),
            P("gz", "gx", "gy", None),
            P(),
        ),
        out_specs=(P(None, None, "gz", "gx", "gy"), P(("gx", "gy", "gz"))),
        check_vma=False,
    )
```

```python
import functools

import jax
import jax.numpy as jnp
from jax import lax
from jax.experimental import pallas as pl
from jax.experimental.pallas import tpu as pltpu
from jax.sharding import PartitionSpec as P

FAC_DEV = 32
TIME_STEP = 0.3
HALF = TIME_STEP
FULL = 2.0 * TIME_STEP
MESH = pl.DeviceIdType.MESH
F32 = jnp.float32


def kernel(sizes, steps, adj, saved, wind, slot, table, impedance, out, grad,
           mid, upp, sav, win, slo, tab, imp, damp, part, prod,
           xs, ys, zs, xr, yr, zr, smat, gs, gr,
           in_sem, x_ss, x_rs, y_ss, y_rs, z_ss, z_rs, g_ss, g_rs):
    nx, ny, nz = sizes
    ix, iy, iz = lax.axis_index("gx"), lax.axis_index("gy"), lax.axis_index("gz")
    right = (lax.rem(ix + 1, nx), iy, iz)
    left = (lax.rem(ix + nx - 1, nx), iy, iz)
    north = (ix, lax.rem(iy + 1, ny), iz)
    south = (ix, lax.rem(iy + ny - 1, ny), iz)
    other = (ix, iy, 1 - iz)
    barrier = pltpu.get_barrier_semaphore()
    for dev in (left, right, south, north, other):
        pl.semaphore_signal(barrier, inc=1, device_id=dev, device_id_type=MESH)

    loads = []
    for i, (src, dst) in enumerate(
        [(wind, win), (adj.at[1], mid), (table.at[0, 0], tab), (slot, slo), (impedance, imp),
         (adj.at[0], upp), (saved, sav)]
    ):
        copy = pltpu.make_async_copy(src, dst, in_sem.at[i])
        copy.start()
        loads.append(copy)

    lane = lax.broadcasted_iota(jnp.int32, (8, 128), 1)
    row = lax.broadcasted_iota(jnp.int32, (8, 128), 0)
    first_row, last_row = row == 0, row == 7
    first_lane, last_lane = lane == 0, lane == 127
    odd = lax.rem(lane, 2) == 1

    def fluxes(c, s, w0, w1, w2):
        own = s[c]
        fz, fx, fy = w0 * own, w1 * own, w2 * own
        if c == 0:
            fz, fx, fy = fz + s[1], fx + s[2], fy + s[3]
        elif c == 1:
            fz = fz + s[0]
        elif c == 2:
            fx = fx + s[0]
        else:
            fy = fy + s[0]
        return fz, fx, fy

    def faces(k, m):
        low = jnp.zeros((8, 128), F32)
        high = jnp.zeros((8, 128), F32)
        allf = [[None] * 8 for _ in range(4)]
        for z in range(8):
            w0, w1, w2 = win[0, z], win[1, z], win[2, z]
            s = [m[c][z] for c in range(4)]
            for c in range(4):
                fz, fx, fy = fluxes(c, s, w0, w1, w2)
                allf[c][z] = (fz, fx, fy)
                n = c * 8 + z
                xs[k, 0, pl.ds(n, 1), :] = fx[0:1]
                xs[k, 1, pl.ds(n, 1), :] = fx[7:8]
                p = 2 * n + 1
                moved = pltpu.roll(fy, p + 1, 1)
                high = jnp.where(lane == p, moved, high)
                low = jnp.where(lane == p + 1, moved, low)
        ys[k, 0] = low
        ys[k, 1] = high
        for c in range(4):
            zs[k, c] = jnp.where(iz == 0, allf[c][7][0], allf[c][0][0])
        return allf

    def copies(k):
        mk = pltpu.make_async_remote_copy
        return [
            mk(src_ref=ys.at[k, 1], dst_ref=yr.at[k, 0], send_sem=y_ss.at[k, 0], recv_sem=y_rs.at[k, 0], device_id=north, device_id_type=MESH),
            mk(src_ref=ys.at[k, 0], dst_ref=yr.at[k, 1], send_sem=y_ss.at[k, 1], recv_sem=y_rs.at[k, 1], device_id=south, device_id_type=MESH),
            mk(src_ref=zs.at[k], dst_ref=zr.at[k], send_sem=z_ss.at[k], recv_sem=z_rs.at[k], device_id=other, device_id_type=MESH),
            mk(src_ref=xs.at[k, 1], dst_ref=xr.at[k, 0], send_sem=x_ss.at[k, 0], recv_sem=x_rs.at[k, 0], device_id=right, device_id_type=MESH),
            mk(src_ref=xs.at[k, 0], dst_ref=xr.at[k, 1], send_sem=x_ss.at[k, 1], recv_sem=x_rs.at[k, 1], device_id=left, device_id_type=MESH),
        ]

    def inner(m, allf, upper):
        for z in range(8):
            d = damp[z] * FULL
            for c in range(4):
                fz, fx, fy = allf[c][z]
                dx = jnp.where(last_row, 0.0, pltpu.roll(fx, 7, 0)) - jnp.where(first_row, 0.0, pltpu.roll(fx, 1, 0))
                dy = jnp.where(last_lane, 0.0, pltpu.roll(fy, 127, 1)) - jnp.where(first_lane, 0.0, pltpu.roll(fy, 1, 1))
                total = dx + dy
                if z < 7:
                    total = total + allf[c][z + 1][0]
                if z > 0:
                    total = total - allf[c][z - 1][0]
                part[c, z] = upper[c][z] + HALF * total - d * m[c][z]

    def finish(k):
        low = jnp.where(iy > 0, -yr[k, 0], 0.0)
        high = jnp.where(iy < ny - 1, pltpu.roll(yr[k, 1], 126, 1), 0.0)
        both = HALF * jnp.where(odd, low, high)
        from_left = jnp.where(ix > 0, -HALF, 0.0)
        from_right = jnp.where(ix < nx - 1, HALF, 0.0)
        top = jnp.where(iz == 0, HALF, 0.0)
        bottom = jnp.where(iz == 0, 0.0, HALF)
        m = [[None] * 8 for _ in range(4)]
        for z in range(8):
            for c in range(4):
                n = c * 8 + z
                value = part[c, z]
                edge = pltpu.roll(both, 128 - (2 * n + 1), 1)
                value = value + jnp.where(first_lane | last_lane, edge, 0.0)
                lrow = xr[k, 0, pl.ds(n, 1), :] * from_left
                rrow = xr[k, 1, pl.ds(n, 1), :] * from_right
                value = value + jnp.where(first_row, lrow, jnp.where(last_row, rrow, 0.0))
                if z == 7:
                    value = value + top * zr[k, c]
                if z == 0:
                    value = value - bottom * zr[k, c]
                m[c][z] = value
        return m

    def add_products(k, m):
        for z in range(8):
            total = m[0][z] * sav[k, 0, z]
            for c in range(1, 4):
                total = total + m[c][z] * sav[k, c, z]
            prod[z] = total if k == 0 else prod[z] + total

    loads[0].wait()
    loads[1].wait()
    m = [[mid[c, z] for z in range(8)] for c in range(4)]
    allf = faces(0, m)
    pl.semaphore_wait(barrier, 5)
    sends = copies(0)
    for copy in sends:
        copy.start()
    everything = list(sends)

    loads[2].wait()
    loads[3].wait()
    loads[4].wait()
    group = iy * nz + iz
    per_row = 128 // FAC_DEV
    stride = (ny * nz) // per_row
    row_of = [lax.rem(ix + o + nx, nx) * stride + group // per_row for o in (0, 1, -1)]
    ids = jnp.broadcast_to(jnp.concatenate([tab[...], tab[...]], axis=1), (8, 128))
    id_row = lax.shift_right_logical(ids, 7)
    id_lane = jnp.bitwise_and(ids, 127)
    lut = jnp.zeros((8, 128), F32)
    for o in range(3):
        line = jnp.broadcast_to(imp[pl.ds(row_of[o], 1), :], (8, 128))
        lut = jnp.where(id_row == row_of[o], jnp.take_along_axis(line, id_lane, axis=1), lut)
    place = jnp.where(id_row == row_of[0], 0, jnp.where(id_row == row_of[1], 32, 64)) + jnp.bitwise_and(ids, 31)
    for z in range(8):
        names = slo[z]
        value = jnp.take_along_axis(lut, jnp.maximum(names - 1, 0), axis=1)
        damp[z] = jnp.where(names > 0, value, 0.0)

    loads[5].wait()
    inner(m, allf, [[upp[c, z] for z in range(8)] for c in range(4)])
    loads[6].wait()
    add_products(0, m)

    older = m
    for k in range(steps):
        for copy in sends:
            copy.wait_recv()
        new = finish(k)
        if k == steps - 1:
            for c in range(4):
                for z in range(8):
                    out[1, c, z] = new[c][z]
            break
        for c in range(4):
            for z in range(8):
                if k == steps - 2:
                    out[0, c, z] = new[c][z]
        allf = faces(k + 1, new)
        sends = copies(k + 1)
        for copy in sends:
            copy.start()
        everything += sends
        add_products(k + 1, new)
        if k == steps - 2:
            for s in range(64):
                total = jnp.zeros((8, 128), F32)
                for z in range(8):
                    total = total + jnp.where(slo[z] == s + 1, prod[z], 0.0)
                smat[pl.ds(s, 1), :] = jnp.sum(total, axis=0, keepdims=True)
            sums = jnp.sum(smat[...], axis=1, keepdims=True) * (-FULL)
            turned = jnp.transpose(jnp.broadcast_to(place[0:1], (128, 128)))[0:64]
            wide = lax.broadcasted_iota(jnp.int32, (64, 128), 1)
            facades = jnp.sum(jnp.where(turned == wide, sums, 0.0), axis=0, keepdims=True)
            gs[...] = jnp.broadcast_to(facades, (8, 128))
            g_sends = [
                pltpu.make_async_remote_copy(src_ref=gs, dst_ref=gr.at[0], send_sem=g_ss.at[0], recv_sem=g_rs.at[0], device_id=right, device_id_type=MESH),
                pltpu.make_async_remote_copy(src_ref=gs, dst_ref=gr.at[1], send_sem=g_ss.at[1], recv_sem=g_rs.at[1], device_id=left, device_id_type=MESH),
            ]
            for copy in g_sends:
                copy.start()
        inner(new, allf, older)
        older = new
    for copy in g_sends:
        copy.wait_recv()
    total = gs[...] + pltpu.roll(gr[0], 96, 1) + pltpu.roll(gr[1], 64, 1)
    grad[...] = total[0, 0:FAC_DEV]
    for copy in everything + g_sends:
        copy.wait_send()


def local(sizes, adjoint, saved_state, wind_field, facade_slot, facade_table, impedance):
    steps = saved_state.shape[0]
    imp = impedance.reshape(-1, 128)
    hbm_spec = pl.BlockSpec(memory_space=pltpu.HBM)
    vmem_spec = pl.BlockSpec(memory_space=pltpu.VMEM)
    v = pltpu.VMEM
    dma = pltpu.SemaphoreType.DMA
    out, grad = pl.pallas_call(
        functools.partial(kernel, sizes, steps),
        out_shape=[
            jax.ShapeDtypeStruct(adjoint.shape, F32),
            jax.ShapeDtypeStruct((FAC_DEV,), F32),
        ],
        in_specs=[hbm_spec] * 6,
        out_specs=[vmem_spec, vmem_spec],
        scratch_shapes=[
            v((4, 8, 8, 128), F32),
            v((4, 8, 8, 128), F32),
            v((steps, 4, 8, 8, 128), F32),
            v((3, 8, 8, 128), F32),
            v((8, 8, 128), jnp.int32),
            v((1, 64), jnp.int32),
            v((128, 128), F32),
            v((8, 8, 128), F32),
            v((4, 8, 8, 128), F32),
            v((8, 8, 128), F32),
            v((steps, 2, 32, 128), F32),
            v((steps, 2, 8, 128), F32),
            v((steps, 4, 8, 128), F32),
            v((steps, 2, 32, 128), F32),
            v((steps, 2, 8, 128), F32),
            v((steps, 4, 8, 128), F32),
            v((64, 128), F32),
            v((8, 128), F32),
            v((2, 8, 128), F32),
            dma((7,)),
            dma((steps, 2)), dma((steps, 2)), dma((steps, 2)), dma((steps, 2)),
            dma((steps,)), dma((steps,)), dma((2,)), dma((2,)),
        ],
        compiler_params=pltpu.CompilerParams(
            collective_id=0, has_side_effects=True, vmem_limit_bytes=32 << 20
        ),
    )(*[pltpu.with_memory_space_constraint(a, pltpu.HBM)
        for a in (adjoint, saved_state, wind_field, facade_slot, facade_table, imp)])
    return out, grad


def solution(mesh):
    sizes = tuple(mesh.shape[a] for a in ("gx", "gy", "gz"))
    return jax.shard_map(
        functools.partial(local, sizes),
        mesh=mesh,
        in_specs=(
            P(None, None, "gz", "gx", "gy"),
            P(None, None, "gz", "gx", "gy"),
            P(None, "gz", "gx", "gy"),
            P("gz", "gx", "gy"),
            P("gz", "gx", "gy", None),
            P(),
        ),
        out_specs=(P(None, None, "gz", "gx", "gy"), P(("gx", "gy", "gz"))),
        check_vma=False,
    )
```

```python
import functools

import jax
import jax.numpy as jnp
from jax import lax
from jax.experimental import pallas as pl
from jax.experimental.pallas import tpu as pltpu
from jax.sharding import PartitionSpec as P

FAC_DEV = 32
TIME_STEP = 0.3
HALF = TIME_STEP
FULL = 2.0 * TIME_STEP
MESH = pl.DeviceIdType.MESH
F32 = jnp.float32

WIND, DAMP, FIELDS = 8, 11, 12
OWN, XH, YH, XYH = 0, 1, 2, 3


def when(cond, run):
    if cond is None:
        run()
    else:
        pl.when(cond)(run)


class Sent:
    def __init__(self, src, dst, send_sem, recv_sem, to, send_if=None, recv_if=None):
        self.copy = pltpu.make_async_remote_copy(
            src_ref=src, dst_ref=dst, send_sem=send_sem, recv_sem=recv_sem, device_id=to, device_id_type=MESH
        )
        self.send_if, self.recv_if = send_if, recv_if

    def start(self):
        when(self.send_if, self.copy.start)

    def wait_recv(self):
        when(self.recv_if, self.copy.wait_recv)

    def wait_send(self):
        when(self.send_if, self.copy.wait_send)


def kernel(sizes, adj, saved, wind, slot, table, impedance, out, grad,
           mid, upp, sav, win, slo, tab, imp, ext, part, prod,
           xbuf, ybuf, zbuf, xr, xzr, yr, yzr, zr, xyr, xyzr,
           xs, ys, zs, xf, yf, zf, smat, gs, gr,
           in_sem, ss, rs, fs, fr, g_ss, g_rs):
    nx, ny, nz = sizes
    ix, iy, iz = lax.axis_index("gx"), lax.axis_index("gy"), lax.axis_index("gz")
    has_right, has_left = ix < nx - 1, ix > 0

    def device(dx, dy, dz):
        return (
            lax.rem(ix + dx + nx, nx) if dx else ix,
            lax.rem(iy + dy + ny, ny) if dy else iy,
            1 - iz if dz else iz,
        )

    barrier = pltpu.get_barrier_semaphore()
    for dx in (0, 1, -1):
        def greet(dx=dx):
            for dy in (0, 1, -1):
                for dz in (1, 0):
                    if dx or dy or dz:
                        pl.semaphore_signal(barrier, inc=1, device_id=device(dx, dy, dz), device_id_type=MESH)

        when({0: None, 1: has_right, -1: has_left}[dx], greet)

    loads = []
    for i, (src, dst) in enumerate(
        [(table.at[0, 0], tab), (impedance, imp), (slot, slo), (wind, win), (adj.at[1], mid), (adj.at[0], upp), (saved, sav)]
    ):
        copy = pltpu.make_async_copy(src, dst, in_sem.at[i])
        copy.start()
        loads.append(copy)

    lane = lax.broadcasted_iota(jnp.int32, (8, 128), 1)
    row = lax.broadcasted_iota(jnp.int32, (8, 128), 0)
    row0, row7, lane0, lane127 = row == 0, row == 7, lane == 0, lane == 127
    quarter = jnp.bitwise_and(lane, 3)
    x_in = ((row < 4) & has_right) | ((row >= 4) & has_left)
    y_in = ((lane < 64) & (iy < ny - 1)) | ((lane >= 64) & (iy > 0))
    inside = {OWN: None, XH: x_in, YH: y_in, XYH: x_in & y_in}
    flipped = iz == 1
    hz = jnp.where(flipped, -HALF, HALF)

    def plane(z):
        return jnp.where(flipped, 7 - z, z)

    def put(f, z, t, value):
        ext[(f * 10 + z) * 4 + t] = value

    def get(f, z, t):
        return ext[(f * 10 + z) * 4 + t]

    for i in range(3):
        loads[i].wait()
    group = iy * nz + iz
    per_row = 128 // FAC_DEV
    stride = (ny * nz) // per_row
    row_of = [lax.rem(ix + o + nx, nx) * stride + group // per_row for o in (0, 1, -1)]
    ids = jnp.broadcast_to(jnp.concatenate([tab[...], tab[...]], axis=1), (8, 128))
    id_row = lax.shift_right_logical(ids, 7)
    id_lane = jnp.bitwise_and(ids, 127)
    lut = jnp.zeros((8, 128), F32)
    for o in range(3):
        line = jnp.broadcast_to(imp[pl.ds(row_of[o], 1), :], (8, 128))
        lut = jnp.where(id_row == row_of[o], jnp.take_along_axis(line, id_lane, axis=1), lut)
    lut = lut * FULL
    place = jnp.where(id_row == row_of[0], 0, jnp.where(id_row == row_of[1], 32, 64)) + jnp.bitwise_and(ids, 31)
    for z in range(8):
        names = slo[plane(z)]
        value = jnp.take_along_axis(lut, jnp.maximum(names - 1, 0), axis=1)
        put(DAMP, z, OWN, jnp.where(names > 0, value, 0.0))
    for i in range(3, 6):
        loads[i].wait()

    def fluxes(s, w):
        fz = [w[0] * v for v in s]
        fx = [w[1] * v for v in s]
        fy = [w[2] * v for v in s]
        fz[0], fz[1] = fz[0] + s[1], fz[1] + s[0]
        fx[0], fx[2] = fx[0] + s[2], fx[2] + s[0]
        fy[0], fy[3] = fy[0] + s[3], fy[3] + s[0]
        return fz, fx, fy

    zero = jnp.zeros((8, 128), F32)
    y_high, y_low = [zero] * 4, [zero] * 4
    for z in reversed(range(8)):
        zi = plane(z)
        own = [mid[c, zi] for c in range(4)] + [upp[c, zi] for c in range(4)] + [win[c, zi] for c in range(3)]
        own.append(get(DAMP, z, OWN))
        for f in range(FIELDS):
            value = own[f]
            if f < DAMP:
                put(f, z, OWN, value)
            if z >= 6:
                zbuf[(7 - z) * FIELDS + f] = value
            n = (7 - z) * FIELDS + f
            k = n % 4
            if k == 0:
                x_high = x_low = zero
            moved = pltpu.roll(value, (2 * k + 2) % 8, 0)
            pair, k_next = row // 2, (k + 1) % 4
            x_high = jnp.where(pair == k, moved, x_high)
            x_low = jnp.where(pair == k_next, moved, x_low)
            if k == 3:
                xbuf[0, n // 4] = x_high
                xbuf[1, n // 4] = x_low
            t, k = n // 32, n % 32
            moved = pltpu.roll(value, (4 * k + 2) % 128, 1)
            quad = lane // 4 == k
            y_high[t] = jnp.where(quad & (quarter < 2), moved, y_high[t])
            y_low[t] = jnp.where(quad & (quarter >= 2), moved, y_low[t])
        fz, fx, fy = fluxes(own[:4], own[8:11])
        for c in range(4):
            if z == 5:
                zbuf[2 * FIELDS + c] = fz[c]
            xbuf[0, 24 + c, pl.ds(z, 1), :] = fx[c][5:6]
            xbuf[1, 24 + c, pl.ds(z, 1), :] = fx[c][2:3]
            k = c * 8 + z
            moved = pltpu.roll(fy[c], (4 * k + 3) % 128, 1)
            y_high[3] = jnp.where(lane == 4 * k, moved, y_high[3])
            y_low[3] = jnp.where(lane == (4 * k + 5) % 128, moved, y_low[3])
    for t in range(4):
        ybuf[0, t] = y_high[t]
        ybuf[1, t] = y_low[t]

    halo = []

    def post(src, dst, to, dx=0):
        i = len(halo)
        send_if, recv_if = {0: (None, None), 1: (has_right, has_left), -1: (has_left, has_right)}[dx]
        halo.append(Sent(src, dst, ss.at[i], rs.at[i], to, send_if, recv_if))

    post(zbuf, zr, device(0, 0, 1))
    for side, d in ((0, 1), (1, -1)):
        post(xbuf.at[side], xr.at[side], device(d, 0, 0), d)
        post(xbuf.at[side, pl.ds(0, 6)], xzr.at[side], device(d, 0, 1), d)
        post(ybuf.at[side], yr.at[side], device(0, d, 0))
        post(ybuf.at[side, 0], yzr.at[side], device(0, d, 1))
        for x_side, e in ((0, 1), (1, -1)):
            post(ybuf.at[side, pl.ds(0, 3)], xyr.at[x_side, side], device(e, d, 0), e)
            post(ybuf.at[side, 0], xyzr.at[x_side, side], device(e, d, 1), e)

    @pl.when(has_left & has_right)
    def _():
        pl.semaphore_wait(barrier, 17)

    @pl.when(ix == 0)
    def _():
        pl.semaphore_wait(barrier, 11)
        pl.semaphore_signal(barrier, inc=1, device_id=(nx - 1, iy, iz), device_id_type=MESH)

    @pl.when(ix == nx - 1)
    def _():
        pl.semaphore_wait(barrier, 12)
        pl.semaphore_signal(barrier, inc=1, device_id=(0, iy, iz), device_id_type=MESH)

    for sent in halo:
        sent.start()

    def add_products(k, base):
        for z in range(8):
            zi = plane(z)
            total = get(base, z, OWN) * sav[k, 0, zi]
            for c in range(1, 4):
                total = total + get(base + c, z, OWN) * sav[k, c, zi]
            prod[z] = total if k == 0 else prod[z] + total

    loads[6].wait()
    add_products(0, 0)
    for sent in halo:
        sent.wait_recv()

    def masked(f, t, value):
        if f < 4 or WIND <= f < DAMP:
            return jnp.where(inside[t], value, 0.0)
        return value

    def both_y(high, low):
        return jnp.where(quarter < 2, high, low)

    y_own = [both_y(yr[0, t], yr[1, t]) for t in range(3)]
    y_top = both_y(yzr[0], yzr[1])
    xy_own = [jnp.where(row < 4, both_y(xyr[1, 0, t], xyr[1, 1, t]), both_y(xyr[0, 0, t], xyr[0, 1, t])) for t in range(3)]
    xy_top = jnp.where(row < 4, both_y(xyzr[1, 0], xyzr[1, 1]), both_y(xyzr[0, 0], xyzr[0, 1]))
    for z in range(10):
        for f in range(FIELDS):
            top = z >= 8
            light = f < 4 or WIND <= f < DAMP
            n = ((z - 8) if top else (7 - z)) * FIELDS + f
            if top:
                put(f, z, OWN, zr[n])
            if z == 9 and not light:
                continue
            src = xzr if top else xr
            k = n % 4
            value = jnp.where(row // 2 == k, src[0, n // 4], src[1, n // 4])
            put(f, z, XH, masked(f, XH, pltpu.roll(value, (6 - 2 * k) % 8, 0)))
            t, k = n // 32, n % 32
            shift = (126 - 4 * k) % 128
            put(f, z, YH, masked(f, YH, pltpu.roll(y_top if top else y_own[t], shift, 1)))
            if z < 8 or (z == 8 and light):
                put(f, z, XYH, masked(f, XYH, pltpu.roll(xy_top if top else xy_own[t], shift, 1)))

    def across(own, far, r_up, r_dn, axis):
        size = own.shape[axis]
        up, dn = size - 1, 1
        own_up, own_dn = pltpu.roll(own, up, axis), pltpu.roll(own, dn, axis)
        far_up, far_dn = pltpu.roll(far, up, axis), pltpu.roll(far, dn, axis)
        return (
            jnp.where(r_up, far_up, own_up) - jnp.where(r_dn, far_dn, own_dn),
            jnp.where(r_up, own_up, far_up) - jnp.where(r_dn, own_dn, far_dn),
        )

    y_flux = jnp.where(quarter == 0, yr[0, 3], yr[1, 3])
    y_third = (lane == 125) | (lane == 2)

    def flux_plane(src, z, tiles, first):
        result = {}
        for t in tiles:
            fz, fx, fy = fluxes([get(src + c, z, t) for c in range(4)], [get(WIND + c, z, t) for c in range(3)])
            if first and z < 8 and t == XH:
                for c in range(4):
                    lo = xr[0, 24 + c, pl.ds(z, 1), :]
                    hi = xr[1, 24 + c, pl.ds(z, 1), :]
                    fx[c] = jnp.where(row == 5, lo, jnp.where(row == 2, hi, fx[c]))
            if first and z < 8 and t == YH:
                for c in range(4):
                    k = c * 8 + z
                    fy[c] = jnp.where(y_third, pltpu.roll(y_flux, (125 - 4 * k) % 128, 1), fy[c])
            result[t] = (fz, fx, fy)
        return result

    def step(src, dst, flux_tiles, new_tiles, top_flux=None, keep=None):
        count = len(flux_tiles)
        first = top_flux is not None
        before, here = None, flux_plane(src, 0, flux_tiles[0], first)
        for z in range(len(new_tiles)):
            after = flux_plane(src, z + 1, flux_tiles[z + 1], first) if z + 1 < count else None
            for c in range(4):
                f = {t: here[t] for t in flux_tiles[z]}
                dx, dy = {}, {}
                dx[OWN], dx[XH] = across(f[OWN][1][c], f[XH][1][c], row7, row0, 0)
                dy[OWN], dy[YH] = across(f[OWN][2][c], f[YH][2][c], lane127, lane0, 1)
                if XYH in f:
                    dx[YH], dx[XYH] = across(f[YH][1][c], f[XYH][1][c], row7, row0, 0)
                    dy[XH], dy[XYH] = across(f[XH][2][c], f[XYH][2][c], lane127, lane0, 1)
                for t in new_tiles[z]:
                    up = after[t][0][c] if after is not None else top_flux[c]
                    dz = up if before is None else up - before[t][0][c]
                    value = get(dst + c, z, t) + HALF * (dx[t] + dy[t]) + hz * dz - get(DAMP, z, t) * get(src + c, z, t)
                    if t != OWN:
                        value = jnp.where(inside[t], value, 0.0)
                    put(dst + c, z, t, value)
                    if keep is not None:
                        keep(c, z, value)
            before, here = here, after

    every = [OWN, XH, YH, XYH]
    sides = [OWN, XH, YH]
    step(0, 4, [every] * 9 + [sides], [every] * 8 + [sides, [OWN]], [zr[2 * FIELDS + c] for c in range(4)])
    add_products(1, 4)
    step(4, 0, [every] * 8 + [sides, [OWN]], [sides] * 8 + [[OWN]])
    add_products(2, 0)
    third = [[None] * 8 for _ in range(4)]

    def keep(c, z, value):
        third[c][z] = value
        out[0, c, plane(z)] = value

    step(0, 4, [sides] * 8 + [[OWN]], [[OWN]] * 8, None, keep)

    low, high = zero, zero
    allf = []
    for z in range(8):
        fz, fx, fy = fluxes([third[c][z] for c in range(4)], [get(WIND + c, z, OWN) for c in range(3)])
        allf.append((fz, fx, fy))
        for c in range(4):
            n = c * 8 + z
            xs[0, pl.ds(n, 1), :] = fx[c][7:8]
            xs[1, pl.ds(n, 1), :] = fx[c][0:1]
            p = 2 * n + 1
            moved = pltpu.roll(fy[c], (p + 1) % 128, 1)
            high = jnp.where(lane == p, moved, high)
            low = jnp.where(lane == (p + 1) % 128, moved, low)
    ys[0], ys[1] = high, low
    for c in range(4):
        zs[c] = allf[7][0][c]
    faces = [
        Sent(ys.at[0], yf.at[0], fs.at[0], fr.at[0], device(0, 1, 0)),
        Sent(ys.at[1], yf.at[1], fs.at[1], fr.at[1], device(0, -1, 0)),
        Sent(zs, zf, fs.at[2], fr.at[2], device(0, 0, 1)),
        Sent(xs.at[0], xf.at[0], fs.at[3], fr.at[3], device(1, 0, 0), has_right, has_left),
        Sent(xs.at[1], xf.at[1], fs.at[4], fr.at[4], device(-1, 0, 0), has_left, has_right),
    ]
    for sent in faces:
        sent.start()
    add_products(3, 4)

    for s in range(64):
        total = zero
        for z in range(8):
            total = total + jnp.where(slo[plane(z)] == s + 1, prod[z], 0.0)
        smat[pl.ds(s, 1), :] = jnp.sum(total, axis=0, keepdims=True)
    sums = jnp.sum(smat[...], axis=1, keepdims=True) * (-FULL)
    turned = jnp.transpose(jnp.broadcast_to(place[0:1], (128, 128)))[0:64]
    wide = lax.broadcasted_iota(jnp.int32, (64, 128), 1)
    facades = jnp.sum(jnp.where(turned == wide, sums, 0.0), axis=0, keepdims=True)
    gs[...] = jnp.broadcast_to(facades, (8, 128))

    @pl.when(ix == 0)
    def _():
        pl.semaphore_wait(barrier, 1)

    parts = [
        Sent(gs, gr.at[0], g_ss.at[0], g_rs.at[0], device(1, 0, 0)),
        Sent(gs, gr.at[1], g_ss.at[1], g_rs.at[1], device(-1, 0, 0)),
    ]
    for sent in parts:
        sent.start()

    for z in range(8):
        d = get(DAMP, z, OWN)
        for c in range(4):
            fz, fx, fy = (allf[z][i][c] for i in range(3))
            dx = jnp.where(row7, 0.0, pltpu.roll(fx, 7, 0)) - jnp.where(row0, 0.0, pltpu.roll(fx, 1, 0))
            dy = jnp.where(lane127, 0.0, pltpu.roll(fy, 127, 1)) - jnp.where(lane0, 0.0, pltpu.roll(fy, 1, 1))
            value = get(c, z, OWN) + HALF * (dx + dy) - d * third[c][z]
            if z < 7:
                value = value + hz * allf[z + 1][0][c]
            if z > 0:
                value = value - hz * allf[z - 1][0][c]
            part[c * 8 + z] = value

    for sent in faces:
        sent.wait_recv()
    south = jnp.where(iy > 0, -yf[0], 0.0)
    north = jnp.where(iy < ny - 1, pltpu.roll(yf[1], 126, 1), 0.0)
    rim = HALF * jnp.where(jnp.bitwise_and(lane, 1) == 1, south, north)
    at_left, at_right = row0 & has_left, row7 & has_right
    for z in range(8):
        for c in range(4):
            n = c * 8 + z
            value = part[n]
            edge = pltpu.roll(rim, 128 - (2 * n + 1), 1)
            value = value + jnp.where(lane0 | lane127, edge, 0.0)
            lrow = xf[0, pl.ds(n, 1), :] * (-HALF)
            rrow = xf[1, pl.ds(n, 1), :] * HALF
            value = value + jnp.where(at_left, lrow, jnp.where(at_right, rrow, 0.0))
            if z == 7:
                value = value + hz * zf[c]
            out[1, c, plane(z)] = value
    for sent in parts:
        sent.wait_recv()
    total = gs[...] + pltpu.roll(gr[0], 96, 1) + pltpu.roll(gr[1], 64, 1)
    grad[...] = total[0, 0:FAC_DEV]
    for sent in halo + faces + parts:
        sent.wait_send()


def local(sizes, adjoint, saved_state, wind_field, facade_slot, facade_table, impedance):
    imp = impedance.reshape(-1, 128)
    hbm_spec = pl.BlockSpec(memory_space=pltpu.HBM)
    vmem_spec = pl.BlockSpec(memory_space=pltpu.VMEM)
    v = pltpu.VMEM
    dma = pltpu.SemaphoreType.DMA
    steps = saved_state.shape[0]
    assert steps == 4
    out, grad = pl.pallas_call(
        functools.partial(kernel, sizes),
        out_shape=[
            jax.ShapeDtypeStruct(adjoint.shape, F32),
            jax.ShapeDtypeStruct((FAC_DEV,), F32),
        ],
        in_specs=[hbm_spec] * 6,
        out_specs=[vmem_spec, vmem_spec],
        scratch_shapes=[
            v((4, 8, 8, 128), F32),
            v((4, 8, 8, 128), F32),
            v((steps, 4, 8, 8, 128), F32),
            v((3, 8, 8, 128), F32),
            v((8, 8, 128), jnp.int32),
            v((1, 64), jnp.int32),
            v((128, 128), F32),
            v((FIELDS * 10 * 4, 8, 128), F32),
            v((32, 8, 128), F32),
            v((8, 8, 128), F32),
            v((2, 28, 8, 128), F32),
            v((2, 4, 8, 128), F32),
            v((28, 8, 128), F32),
            v((2, 28, 8, 128), F32),
            v((2, 6, 8, 128), F32),
            v((2, 4, 8, 128), F32),
            v((2, 8, 128), F32),
            v((28, 8, 128), F32),
            v((2, 2, 3, 8, 128), F32),
            v((2, 2, 8, 128), F32),
            v((2, 32, 128), F32),
            v((2, 8, 128), F32),
            v((4, 8, 128), F32),
            v((2, 32, 128), F32),
            v((2, 8, 128), F32),
            v((4, 8, 128), F32),
            v((64, 128), F32),
            v((8, 128), F32),
            v((2, 8, 128), F32),
            dma((7,)), dma((17,)), dma((17,)), dma((5,)), dma((5,)), dma((2,)), dma((2,)),
        ],
        compiler_params=pltpu.CompilerParams(
            collective_id=0, has_side_effects=True, vmem_limit_bytes=32 << 20
        ),
    )(*[pltpu.with_memory_space_constraint(a, pltpu.HBM)
        for a in (adjoint, saved_state, wind_field, facade_slot, facade_table, imp)])
    return out, grad


def solution(mesh):
    sizes = tuple(mesh.shape[a] for a in ("gx", "gy", "gz"))
    return jax.shard_map(
        functools.partial(local, sizes),
        mesh=mesh,
        in_specs=(
            P(None, None, "gz", "gx", "gy"),
            P(None, None, "gz", "gx", "gy"),
            P(None, "gz", "gx", "gy"),
            P("gz", "gx", "gy"),
            P("gz", "gx", "gy", None),
            P(),
        ),
        out_specs=(P(None, None, "gz", "gx", "gy"), P(("gx", "gy", "gz"))),
        check_vma=False,
    )
```

```python
import functools

import jax
import jax.numpy as jnp
from jax import lax
from jax.experimental import pallas as pl
from jax.experimental.pallas import tpu as pltpu
from jax.sharding import PartitionSpec as P

FAC_DEV = 32
TIME_STEP = 0.3
HALF = TIME_STEP
FULL = 2.0 * TIME_STEP
MESH = pl.DeviceIdType.MESH
F32 = jnp.float32

WIND, DAMP, FIELDS = 8, 11, 12
OWN, XH, YH, XYH = 0, 1, 2, 3


def when(cond, run):
    if cond is None:
        run()
    else:
        pl.when(cond)(run)


class Sent:
    def __init__(self, src, dst, send_sem, recv_sem, to, send_if=None, recv_if=None):
        self.copy = pltpu.make_async_remote_copy(
            src_ref=src, dst_ref=dst, send_sem=send_sem, recv_sem=recv_sem, device_id=to, device_id_type=MESH
        )
        self.send_if, self.recv_if = send_if, recv_if

    def start(self):
        when(self.send_if, self.copy.start)

    def wait_recv(self):
        when(self.recv_if, self.copy.wait_recv)

    def wait_send(self):
        when(self.send_if, self.copy.wait_send)


def kernel(sizes, adj, saved, wind, slot, table, impedance, out, grad,
           mid, upp, sav, win, slo, tab, imp, ext, part, prod,
           xbuf, xzbuf, ybuf, xybuf, zbuf, xr, xzr, yr, yzr, zr, xyr, xyzr,
           xs, ys, zs, xf, yf, zf, smat, gs, gr,
           in_sem, ss, rs, fs, fr, g_ss, g_rs):
    nx, ny, nz = sizes
    ix, iy, iz = lax.axis_index("gx"), lax.axis_index("gy"), lax.axis_index("gz")
    has_right, has_left = ix < nx - 1, ix > 0

    def device(dx, dy, dz):
        return (
            lax.rem(ix + dx + nx, nx) if dx else ix,
            lax.rem(iy + dy + ny, ny) if dy else iy,
            1 - iz if dz else iz,
        )

    barrier = pltpu.get_barrier_semaphore()
    for dx in (0, 1, -1):
        def greet(dx=dx):
            for dy in (0, 1, -1):
                for dz in (1, 0):
                    if dx or dy or dz:
                        pl.semaphore_signal(barrier, inc=1, device_id=device(dx, dy, dz), device_id_type=MESH)

        when({0: None, 1: has_right, -1: has_left}[dx], greet)

    loads = []
    for i, (src, dst) in enumerate(
        [(table.at[0, 0], tab), (impedance, imp), (slot, slo), (wind, win), (adj.at[1], mid), (adj.at[0], upp), (saved, sav)]
    ):
        copy = pltpu.make_async_copy(src, dst, in_sem.at[i])
        copy.start()
        loads.append(copy)

    lane = lax.broadcasted_iota(jnp.int32, (8, 128), 1)
    row = lax.broadcasted_iota(jnp.int32, (8, 128), 0)
    row0, row7, lane0, lane127 = row == 0, row == 7, lane == 0, lane == 127
    quarter = jnp.bitwise_and(lane, 3)
    x_in = ((row < 4) & has_right) | ((row >= 4) & has_left)
    y_in = ((lane < 64) & (iy < ny - 1)) | ((lane >= 64) & (iy > 0))
    inside = {OWN: None, XH: x_in, YH: y_in, XYH: x_in & y_in}
    flipped = iz == 1
    hz = jnp.where(flipped, -HALF, HALF)

    def plane(z):
        return jnp.where(flipped, 7 - z, z)

    def put(f, z, t, value):
        ext[(f * 10 + z) * 4 + t] = value

    def get(f, z, t):
        return ext[(f * 10 + z) * 4 + t]

    for i in range(3):
        loads[i].wait()
    group = iy * nz + iz
    per_row = 128 // FAC_DEV
    stride = (ny * nz) // per_row
    row_of = [lax.rem(ix + o + nx, nx) * stride + group // per_row for o in (0, 1, -1)]
    ids = jnp.broadcast_to(jnp.concatenate([tab[...], tab[...]], axis=1), (8, 128))
    id_row = lax.shift_right_logical(ids, 7)
    id_lane = jnp.bitwise_and(ids, 127)
    lut = jnp.zeros((8, 128), F32)
    for o in range(3):
        line = jnp.broadcast_to(imp[pl.ds(row_of[o], 1), :], (8, 128))
        lut = jnp.where(id_row == row_of[o], jnp.take_along_axis(line, id_lane, axis=1), lut)
    lut = lut * FULL
    place = jnp.where(id_row == row_of[0], 0, jnp.where(id_row == row_of[1], 32, 64)) + jnp.bitwise_and(ids, 31)
    for z in range(8):
        names = slo[plane(z)]
        value = jnp.take_along_axis(lut, jnp.maximum(names - 1, 0), axis=1)
        put(DAMP, z, OWN, jnp.where(names > 0, value, 0.0))
    for i in range(3, 6):
        loads[i].wait()

    def fluxes(s, w):
        fz = [w[0] * v for v in s]
        fx = [w[1] * v for v in s]
        fy = [w[2] * v for v in s]
        fz[0], fz[1] = fz[0] + s[1], fz[1] + s[0]
        fx[0], fx[2] = fx[0] + s[2], fx[2] + s[0]
        fy[0], fy[3] = fy[0] + s[3], fy[3] + s[0]
        return fz, fx, fy

    zero = jnp.zeros((8, 128), F32)

    def within(level, allf, upper, store):
        for z in range(8):
            d = get(DAMP, z, OWN)
            for c in range(4):
                fz, fx, fy = (allf[z][i][c] for i in range(3))
                dx = jnp.where(row7, 0.0, pltpu.roll(fx, 7, 0)) - jnp.where(row0, 0.0, pltpu.roll(fx, 1, 0))
                dy = jnp.where(lane127, 0.0, pltpu.roll(fy, 127, 1)) - jnp.where(lane0, 0.0, pltpu.roll(fy, 1, 1))
                value = upper(c, z) + HALF * (dx + dy) - d * level(c, z)
                if 0 < z < 7:
                    value = value + hz * (allf[z + 1][0][c] - allf[z - 1][0][c])
                elif z == 0:
                    value = value + hz * allf[1][0][c]
                else:
                    value = value - hz * allf[6][0][c]
                store(c, z, value)

    allf = []
    for z in range(8):
        zi = plane(z)
        own = [mid[c, zi] for c in range(4)]
        wz = [win[c, zi] for c in range(3)]
        for c in range(4):
            put(c, z, OWN, own[c])
        for c in range(3):
            put(WIND + c, z, OWN, wz[c])
        allf.append(fluxes(own, wz))
    within(
        lambda c, z: get(c, z, OWN), allf, lambda c, z: upp[c, plane(z)], lambda c, z, value: put(4 + c, z, OWN, value)
    )

    y_high, y_low = [zero] * 3, [zero] * 3
    for z in reversed(range(8)):
        for f in range(FIELDS):
            value = get(f, z, OWN)
            if z == 7:
                zbuf[f] = value
            if z == 6 and 4 <= f <= WIND:
                zbuf[FIELDS + f - 4] = value
            n = (7 - z) * FIELDS + f
            k = n % 4
            if k == 0:
                x_high = x_low = zero
            moved = pltpu.roll(value, (2 * k + 2) % 8, 0)
            pair, k_next = row // 2, (k + 1) % 4
            x_high = jnp.where(pair == k, moved, x_high)
            x_low = jnp.where(pair == k_next, moved, x_low)
            if k == 3:
                xbuf[0, n // 4] = x_high
                xbuf[1, n // 4] = x_low
            t, k = n // 32, n % 32
            moved = pltpu.roll(value, (4 * k + 2) % 128, 1)
            quad = lane // 4 == k
            y_high[t] = jnp.where(quad & (quarter < 2), moved, y_high[t])
            y_low[t] = jnp.where(quad & (quarter >= 2), moved, y_low[t])
            if z == 7 and f < WIND + 2:
                xzbuf[0, pl.ds(f, 1), :] = value[7:8]
                xzbuf[1, pl.ds(f, 1), :] = value[0:1]
    for c in range(4):
        xzbuf[0, pl.ds(10 + c, 1), :] = allf[7][0][c][6:7]
        xzbuf[1, pl.ds(10 + c, 1), :] = allf[7][0][c][1:2]
        xzbuf[0, pl.ds(14 + c, 1), :] = allf[6][1][c][7:8]
        xzbuf[1, pl.ds(14 + c, 1), :] = allf[6][1][c][0:1]
    for side, tiles in ((0, y_high), (1, y_low)):
        xy_high, xy_low = zero, zero
        for t in range(3):
            ybuf[side, t] = tiles[t]
            moved = pltpu.roll(tiles[t], (2 * t + 2) % 8, 0)
            xy_high = jnp.where(row // 2 == t, moved, xy_high)
            xy_low = jnp.where(row // 2 == t + 1, moved, xy_low)
        xybuf[0, side] = xy_high
        xybuf[1, side] = xy_low

    halo = []

    def post(src, dst, to, dx=0):
        i = len(halo)
        send_if, recv_if = {0: (None, None), 1: (has_right, has_left), -1: (has_left, has_right)}[dx]
        halo.append(Sent(src, dst, ss.at[i], rs.at[i], to, send_if, recv_if))

    post(zbuf, zr, device(0, 0, 1))
    for side, d in ((0, 1), (1, -1)):
        post(xbuf.at[side], xr.at[side], device(d, 0, 0), d)
        post(xzbuf.at[side], xzr.at[side], device(d, 0, 1), d)
        post(ybuf.at[side], yr.at[side], device(0, d, 0))
        post(ybuf.at[side, 0], yzr.at[side], device(0, d, 1))
        for x_side, e in ((0, 1), (1, -1)):
            post(xybuf.at[x_side, side], xyr.at[x_side, side], device(e, d, 0), e)
            post(xybuf.at[x_side, side], xyzr.at[x_side, side], device(e, d, 1), e)

    @pl.when(has_left & has_right)
    def _():
        pl.semaphore_wait(barrier, 17)

    @pl.when(ix == 0)
    def _():
        pl.semaphore_wait(barrier, 11)
        pl.semaphore_signal(barrier, inc=1, device_id=(nx - 1, iy, iz), device_id_type=MESH)

    @pl.when(ix == nx - 1)
    def _():
        pl.semaphore_wait(barrier, 12)
        pl.semaphore_signal(barrier, inc=1, device_id=(0, iy, iz), device_id_type=MESH)

    for sent in halo:
        sent.start()

    def add_products(k, base):
        for z in range(8):
            zi = plane(z)
            total = get(base, z, OWN) * sav[k, 0, zi]
            for c in range(1, 4):
                total = total + get(base + c, z, OWN) * sav[k, c, zi]
            prod[z] = total if k == 0 else prod[z] + total

    loads[6].wait()
    add_products(0, 0)
    for sent in halo:
        sent.wait_recv()

    def masked(f, t, value):
        if f < 4 or WIND <= f < DAMP:
            return jnp.where(inside[t], value, 0.0)
        return value

    def both_y(high, low):
        return jnp.where(quarter < 2, high, low)

    y_own = [both_y(yr[0, t], yr[1, t]) for t in range(3)]
    y_top = both_y(yzr[0], yzr[1])

    def xy_tile(src, t):
        value = jnp.where(row // 2 == t, both_y(src[0, 0], src[0, 1]), both_y(src[1, 0], src[1, 1]))
        return pltpu.roll(value, (6 - 2 * t) % 8, 0)

    xy_own = [xy_tile(xyr, t) for t in range(3)]
    xy_top = xy_tile(xyzr, 0)
    for z in range(8):
        for f in range(FIELDS):
            n = (7 - z) * FIELDS + f
            k = n % 4
            value = jnp.where(row // 2 == k, xr[0, n // 4], xr[1, n // 4])
            put(f, z, XH, masked(f, XH, pltpu.roll(value, (6 - 2 * k) % 8, 0)))
            t, k = n // 32, n % 32
            shift = (126 - 4 * k) % 128
            put(f, z, YH, masked(f, YH, pltpu.roll(y_own[t], shift, 1)))
            if f < DAMP:
                put(f, z, XYH, masked(f, XYH, pltpu.roll(xy_own[t], shift, 1)))
    for f in range(FIELDS):
        put(f, 8, OWN, zr[f])
        if 4 <= f <= WIND:
            put(f, 9, OWN, zr[FIELDS + f - 4])
        if f < WIND + 2:
            value = jnp.where(row == 7, xzr[0, pl.ds(f, 1), :], xzr[1, pl.ds(f, 1), :])
            put(f, 8, XH, masked(f, XH, value))
        shift = (126 - 4 * f) % 128
        if f < DAMP:
            put(f, 8, YH, masked(f, YH, pltpu.roll(y_top, shift, 1)))
        if f < 4 or WIND <= f < DAMP:
            put(f, 8, XYH, masked(f, XYH, pltpu.roll(xy_top, shift, 1)))
            put(f, 9, YH, masked(f, YH, pltpu.roll(y_top, (126 - 4 * (FIELDS + f)) % 128, 1)))

    def across(own, far, r_up, r_dn, axis):
        size = own.shape[axis]
        up, dn = size - 1, 1
        own_up, own_dn = pltpu.roll(own, up, axis), pltpu.roll(own, dn, axis)
        far_up, far_dn = pltpu.roll(far, up, axis), pltpu.roll(far, dn, axis)
        return (
            jnp.where(r_up, far_up, own_up) - jnp.where(r_dn, far_dn, own_dn),
            jnp.where(r_up, own_up, far_up) - jnp.where(r_dn, own_dn, far_dn),
        )

    def flux_tile(src, z, t):
        return fluxes([get(src + c, z, t) for c in range(4)], [get(WIND + c, z, t) for c in range(3)])

    def flux_plane(src, z, tiles):
        return {t: flux_tile(src, z, t) for t in tiles}

    def seam(flux, r_up, r_dn, axis):
        size = flux.shape[axis]
        return jnp.where(r_up, pltpu.roll(flux, size - 1, axis), 0.0) - jnp.where(r_dn, pltpu.roll(flux, 1, axis), 0.0)

    def first_step():
        beside_x = {OWN: XH, XH: OWN, YH: XYH, XYH: YH}
        beside_y = {OWN: YH, YH: OWN, XH: XYH, XYH: XH}
        here = None
        after = flux_plane(0, 0, [OWN, XH, YH, XYH])
        for z in range(10):
            before, here = here, after
            after = None
            if z + 1 < 9:
                after = flux_plane(0, z + 1, [OWN, XH, YH, XYH])
                if z + 1 == 8:
                    fz = after[XH][0]
                    for c in range(4):
                        lo, hi = xzr[0, pl.ds(10 + c, 1), :], xzr[1, pl.ds(10 + c, 1), :]
                        fz[c] = jnp.where(row == 6, lo, jnp.where(row == 1, hi, fz[c]))
            elif z + 1 == 9:
                fx = []
                for c in range(4):
                    lo, hi = xzr[0, pl.ds(14 + c, 1), :], xzr[1, pl.ds(14 + c, 1), :]
                    fx.append(jnp.where(inside[XH], jnp.where(row == 7, lo, hi), 0.0))
                after = {XH: (None, fx, None), YH: flux_tile(0, 9, YH)}
            for t in [OWN, XH, YH, XYH] if z < 8 else [OWN, XH, YH] if z == 8 else [OWN]:
                for c in range(4):
                    sx = seam(here[beside_x[t]][1][c], row7, row0, 0)
                    sy = seam(here[beside_y[t]][2][c], lane127, lane0, 1)
                    value = get(4 + c, z, t) + HALF * (sx + sy)
                    if z == 7:
                        value = value + hz * after[t][0][c]
                    if z == 8:
                        value = value - hz * before[t][0][c]
                    if t != OWN:
                        value = jnp.where(inside[t], value, 0.0)
                    put(4 + c, z, t, value)

    def step(src, dst, flux_tiles, new_tiles, keep=None):
        before, here = None, flux_plane(src, 0, flux_tiles[0])
        for z in range(len(new_tiles)):
            after = flux_plane(src, z + 1, flux_tiles[z + 1])
            for c in range(4):
                f = {t: here[t] for t in flux_tiles[z]}
                dx, dy = {}, {}
                dx[OWN], dx[XH] = across(f[OWN][1][c], f[XH][1][c], row7, row0, 0)
                dy[OWN], dy[YH] = across(f[OWN][2][c], f[YH][2][c], lane127, lane0, 1)
                if XYH in f:
                    dx[YH], dx[XYH] = across(f[YH][1][c], f[XYH][1][c], row7, row0, 0)
                    dy[XH], dy[XYH] = across(f[XH][2][c], f[XYH][2][c], lane127, lane0, 1)
                for t in new_tiles[z]:
                    up = after[t][0][c]
                    dz = up if before is None else up - before[t][0][c]
                    value = get(dst + c, z, t) + HALF * (dx[t] + dy[t]) + hz * dz - get(DAMP, z, t) * get(src + c, z, t)
                    if t != OWN:
                        value = jnp.where(inside[t], value, 0.0)
                    put(dst + c, z, t, value)
                    if keep is not None:
                        keep(c, z, value)
            before, here = here, after

    every = [OWN, XH, YH, XYH]
    sides = [OWN, XH, YH]
    first_step()
    add_products(1, 4)
    step(4, 0, [every] * 8 + [sides, [OWN]], [sides] * 8 + [[OWN]])
    add_products(2, 0)
    third = [[None] * 8 for _ in range(4)]

    def keep(c, z, value):
        third[c][z] = value
        out[0, c, plane(z)] = value

    step(0, 4, [sides] * 8 + [[OWN]], [[OWN]] * 8, keep)

    low, high = zero, zero
    allf = []
    for z in range(8):
        fz, fx, fy = fluxes([third[c][z] for c in range(4)], [get(WIND + c, z, OWN) for c in range(3)])
        allf.append((fz, fx, fy))
        for c in range(4):
            n = c * 8 + z
            xs[0, pl.ds(n, 1), :] = fx[c][7:8]
            xs[1, pl.ds(n, 1), :] = fx[c][0:1]
            p = 2 * n + 1
            moved = pltpu.roll(fy[c], (p + 1) % 128, 1)
            high = jnp.where(lane == p, moved, high)
            low = jnp.where(lane == (p + 1) % 128, moved, low)
    ys[0], ys[1] = high, low
    for c in range(4):
        zs[c] = allf[7][0][c]
    faces = [
        Sent(ys.at[0], yf.at[0], fs.at[0], fr.at[0], device(0, 1, 0)),
        Sent(ys.at[1], yf.at[1], fs.at[1], fr.at[1], device(0, -1, 0)),
        Sent(zs, zf, fs.at[2], fr.at[2], device(0, 0, 1)),
        Sent(xs.at[0], xf.at[0], fs.at[3], fr.at[3], device(1, 0, 0), has_right, has_left),
        Sent(xs.at[1], xf.at[1], fs.at[4], fr.at[4], device(-1, 0, 0), has_left, has_right),
    ]
    for sent in faces:
        sent.start()
    add_products(3, 4)

    for s in range(64):
        total = zero
        for z in range(8):
            total = total + jnp.where(slo[plane(z)] == s + 1, prod[z], 0.0)
        smat[pl.ds(s, 1), :] = jnp.sum(total, axis=0, keepdims=True)
    sums = jnp.sum(smat[...], axis=1, keepdims=True) * (-FULL)
    turned = jnp.transpose(jnp.broadcast_to(place[0:1], (128, 128)))[0:64]
    wide = lax.broadcasted_iota(jnp.int32, (64, 128), 1)
    facades = jnp.sum(jnp.where(turned == wide, sums, 0.0), axis=0, keepdims=True)
    gs[...] = jnp.broadcast_to(facades, (8, 128))

    @pl.when(ix == 0)
    def _():
        pl.semaphore_wait(barrier, 1)

    parts = [
        Sent(gs, gr.at[0], g_ss.at[0], g_rs.at[0], device(1, 0, 0)),
        Sent(gs, gr.at[1], g_ss.at[1], g_rs.at[1], device(-1, 0, 0)),
    ]
    for sent in parts:
        sent.start()

    def hold(c, z, value):
        part[c * 8 + z] = value

    within(lambda c, z: third[c][z], allf, lambda c, z: get(c, z, OWN), hold)

    for sent in faces:
        sent.wait_recv()
    south = jnp.where(iy > 0, -yf[0], 0.0)
    north = jnp.where(iy < ny - 1, pltpu.roll(yf[1], 126, 1), 0.0)
    rim = HALF * jnp.where(jnp.bitwise_and(lane, 1) == 1, south, north)
    at_left, at_right = row0 & has_left, row7 & has_right
    for z in range(8):
        for c in range(4):
            n = c * 8 + z
            value = part[n]
            edge = pltpu.roll(rim, 128 - (2 * n + 1), 1)
            value = value + jnp.where(lane0 | lane127, edge, 0.0)
            lrow = xf[0, pl.ds(n, 1), :] * (-HALF)
            rrow = xf[1, pl.ds(n, 1), :] * HALF
            value = value + jnp.where(at_left, lrow, jnp.where(at_right, rrow, 0.0))
            if z == 7:
                value = value + hz * zf[c]
            out[1, c, plane(z)] = value
    for sent in parts:
        sent.wait_recv()
    total = gs[...] + pltpu.roll(gr[0], 96, 1) + pltpu.roll(gr[1], 64, 1)
    grad[...] = total[0, 0:FAC_DEV]
    for sent in halo + faces + parts:
        sent.wait_send()


def local(sizes, adjoint, saved_state, wind_field, facade_slot, facade_table, impedance):
    imp = impedance.reshape(-1, 128)
    hbm_spec = pl.BlockSpec(memory_space=pltpu.HBM)
    vmem_spec = pl.BlockSpec(memory_space=pltpu.VMEM)
    v = pltpu.VMEM
    dma = pltpu.SemaphoreType.DMA
    steps = saved_state.shape[0]
    assert steps == 4
    out, grad = pl.pallas_call(
        functools.partial(kernel, sizes),
        out_shape=[
            jax.ShapeDtypeStruct(adjoint.shape, F32),
            jax.ShapeDtypeStruct((FAC_DEV,), F32),
        ],
        in_specs=[hbm_spec] * 6,
        out_specs=[vmem_spec, vmem_spec],
        scratch_shapes=[
            v((4, 8, 8, 128), F32),
            v((4, 8, 8, 128), F32),
            v((steps, 4, 8, 8, 128), F32),
            v((3, 8, 8, 128), F32),
            v((8, 8, 128), jnp.int32),
            v((1, 64), jnp.int32),
            v((128, 128), F32),
            v((FIELDS * 10 * 4, 8, 128), F32),
            v((32, 8, 128), F32),
            v((8, 8, 128), F32),
            v((2, 24, 8, 128), F32),
            v((2, 24, 128), F32),
            v((2, 3, 8, 128), F32),
            v((2, 2, 8, 128), F32),
            v((17, 8, 128), F32),
            v((2, 24, 8, 128), F32),
            v((2, 24, 128), F32),
            v((2, 3, 8, 128), F32),
            v((2, 8, 128), F32),
            v((17, 8, 128), F32),
            v((2, 2, 8, 128), F32),
            v((2, 2, 8, 128), F32),
            v((2, 32, 128), F32),
            v((2, 8, 128), F32),
            v((4, 8, 128), F32),
            v((2, 32, 128), F32),
            v((2, 8, 128), F32),
            v((4, 8, 128), F32),
            v((64, 128), F32),
            v((8, 128), F32),
            v((2, 8, 128), F32),
            dma((7,)), dma((17,)), dma((17,)), dma((5,)), dma((5,)), dma((2,)), dma((2,)),
        ],
        compiler_params=pltpu.CompilerParams(
            collective_id=0, has_side_effects=True, vmem_limit_bytes=32 << 20
        ),
    )(*[pltpu.with_memory_space_constraint(a, pltpu.HBM)
        for a in (adjoint, saved_state, wind_field, facade_slot, facade_table, imp)])
    return out, grad


def solution(mesh):
    sizes = tuple(mesh.shape[a] for a in ("gx", "gy", "gz"))
    return jax.shard_map(
        functools.partial(local, sizes),
        mesh=mesh,
        in_specs=(
            P(None, None, "gz", "gx", "gy"),
            P(None, None, "gz", "gx", "gy"),
            P(None, "gz", "gx", "gy"),
            P("gz", "gx", "gy"),
            P("gz", "gx", "gy", None),
            P(),
        ),
        out_specs=(P(None, None, "gz", "gx", "gy"), P(("gx", "gy", "gz"))),
        check_vma=False,
    )
```

```python
import functools

import jax
import jax.numpy as jnp
from jax import lax
from jax.experimental import pallas as pl
from jax.experimental.pallas import tpu as pltpu
from jax.sharding import PartitionSpec as P

FAC_DEV = 32
TIME_STEP = 0.3
HALF = TIME_STEP
FULL = 2.0 * TIME_STEP
MESH = pl.DeviceIdType.MESH
F32 = jnp.float32

WIND, DAMP, FIELDS = 8, 11, 12
OWN, XH, YH, XYH = 0, 1, 2, 3


def when(cond, run):
    if cond is None:
        run()
    else:
        pl.when(cond)(run)


class Sent:
    def __init__(self, src, dst, send_sem, recv_sem, to, send_if=None, recv_if=None):
        self.copy = pltpu.make_async_remote_copy(
            src_ref=src, dst_ref=dst, send_sem=send_sem, recv_sem=recv_sem, device_id=to, device_id_type=MESH
        )
        self.send_if, self.recv_if = send_if, recv_if

    def start(self):
        when(self.send_if, self.copy.start)

    def wait_recv(self):
        when(self.recv_if, self.copy.wait_recv)

    def wait_send(self):
        when(self.send_if, self.copy.wait_send)


def kernel(sizes, adj, saved, wind, slot, table, impedance, out, grad,
           mid, upp, sav, win, slo, tab, imp, ext, part, prod,
           xbuf, xzbuf, ybuf, xybuf, zbuf, xr, xzr, yr, yzr, zr, xyr, xyzr,
           xs, ys, zs, xf, yf, zf, slots, smat, gs, gr,
           in_sem, ss, rs, fs, fr, g_ss, g_rs):
    nx, ny, nz = sizes
    ix, iy, iz = lax.axis_index("gx"), lax.axis_index("gy"), lax.axis_index("gz")
    has_right, has_left = ix < nx - 1, ix > 0

    def device(dx, dy, dz):
        return (
            lax.rem(ix + dx + nx, nx) if dx else ix,
            lax.rem(iy + dy + ny, ny) if dy else iy,
            1 - iz if dz else iz,
        )

    barrier = pltpu.get_barrier_semaphore()
    for dx in (0, 1, -1):
        def greet(dx=dx):
            for dy in (0, 1, -1):
                for dz in (1, 0):
                    if dx or dy or dz:
                        pl.semaphore_signal(barrier, inc=1, device_id=device(dx, dy, dz), device_id_type=MESH)

        when({0: None, 1: has_right, -1: has_left}[dx], greet)

    loads = []
    for i, (src, dst) in enumerate(
        [(table.at[0, 0], tab), (impedance, imp), (slot, slo), (wind, win), (adj.at[1], mid), (adj.at[0], upp), (saved, sav)]
    ):
        copy = pltpu.make_async_copy(src, dst, in_sem.at[i])
        copy.start()
        loads.append(copy)

    lane = lax.broadcasted_iota(jnp.int32, (8, 128), 1)
    row = lax.broadcasted_iota(jnp.int32, (8, 128), 0)
    row0, row7, lane0, lane127 = row == 0, row == 7, lane == 0, lane == 127
    quarter = jnp.bitwise_and(lane, 3)
    x_in = ((row < 4) & has_right) | ((row >= 4) & has_left)
    y_in = ((lane < 64) & (iy < ny - 1)) | ((lane >= 64) & (iy > 0))
    inside = {OWN: None, XH: x_in, YH: y_in, XYH: x_in & y_in}
    flipped = iz == 1
    hz = jnp.where(flipped, -HALF, HALF)

    def plane(z):
        return jnp.where(flipped, 7 - z, z)

    def put(f, z, t, value):
        ext[(f * 10 + z) * 4 + t] = value

    def get(f, z, t):
        return ext[(f * 10 + z) * 4 + t]

    for i in range(3):
        loads[i].wait()
    group = iy * nz + iz
    per_row = 128 // FAC_DEV
    stride = (ny * nz) // per_row
    row_of = [lax.rem(ix + o + nx, nx) * stride + group // per_row for o in (0, 1, -1)]
    ids = jnp.broadcast_to(jnp.concatenate([tab[...], tab[...]], axis=1), (8, 128))
    id_row = lax.shift_right_logical(ids, 7)
    id_lane = jnp.bitwise_and(ids, 127)
    lut = jnp.zeros((8, 128), F32)
    for o in range(3):
        line = jnp.broadcast_to(imp[pl.ds(row_of[o], 1), :], (8, 128))
        lut = jnp.where(id_row == row_of[o], jnp.take_along_axis(line, id_lane, axis=1), lut)
    lut = lut * FULL
    place = jnp.where(id_row == row_of[0], 0, jnp.where(id_row == row_of[1], 32, 64)) + jnp.bitwise_and(ids, 31)
    for z in range(8):
        names = slo[plane(z)]
        value = jnp.take_along_axis(lut, jnp.maximum(names - 1, 0), axis=1)
        put(DAMP, z, OWN, jnp.where(names > 0, value, 0.0))
    for i in range(3, 6):
        loads[i].wait()

    def fluxes(s, w):
        fz = [w[0] * v for v in s]
        fx = [w[1] * v for v in s]
        fy = [w[2] * v for v in s]
        fz[0], fz[1] = fz[0] + s[1], fz[1] + s[0]
        fx[0], fx[2] = fx[0] + s[2], fx[2] + s[0]
        fy[0], fy[3] = fy[0] + s[3], fy[3] + s[0]
        return fz, fx, fy

    zero = jnp.zeros((8, 128), F32)

    def within(level, allf, upper, store):
        for z in range(8):
            d = get(DAMP, z, OWN)
            for c in range(4):
                fz, fx, fy = (allf[z][i][c] for i in range(3))
                dx = jnp.where(row7, 0.0, pltpu.roll(fx, 7, 0)) - jnp.where(row0, 0.0, pltpu.roll(fx, 1, 0))
                dy = jnp.where(lane127, 0.0, pltpu.roll(fy, 127, 1)) - jnp.where(lane0, 0.0, pltpu.roll(fy, 1, 1))
                value = upper(c, z) + HALF * (dx + dy) - d * level(c, z)
                if 0 < z < 7:
                    value = value + hz * (allf[z + 1][0][c] - allf[z - 1][0][c])
                elif z == 0:
                    value = value + hz * allf[1][0][c]
                else:
                    value = value - hz * allf[6][0][c]
                store(c, z, value)

    allf = []
    for z in range(8):
        zi = plane(z)
        own = [mid[c, zi] for c in range(4)]
        wz = [win[c, zi] for c in range(3)]
        for c in range(4):
            put(c, z, OWN, own[c])
        for c in range(3):
            put(WIND + c, z, OWN, wz[c])
        allf.append(fluxes(own, wz))
    within(
        lambda c, z: get(c, z, OWN), allf, lambda c, z: upp[c, plane(z)], lambda c, z, value: put(4 + c, z, OWN, value)
    )

    y_high, y_low = [zero] * 3, [zero] * 3
    for z in reversed(range(8)):
        for f in range(FIELDS):
            value = get(f, z, OWN)
            if z == 7:
                zbuf[f] = value
            if z == 6 and 4 <= f <= WIND:
                zbuf[FIELDS + f - 4] = value
            n = (7 - z) * FIELDS + f
            k = n % 4
            if k == 0:
                x_high = x_low = zero
            moved = pltpu.roll(value, (2 * k + 2) % 8, 0)
            pair, k_next = row // 2, (k + 1) % 4
            x_high = jnp.where(pair == k, moved, x_high)
            x_low = jnp.where(pair == k_next, moved, x_low)
            if k == 3:
                xbuf[0, n // 4] = x_high
                xbuf[1, n // 4] = x_low
            t, k = n // 32, n % 32
            moved = pltpu.roll(value, (4 * k + 2) % 128, 1)
            quad = lane // 4 == k
            y_high[t] = jnp.where(quad & (quarter < 2), moved, y_high[t])
            y_low[t] = jnp.where(quad & (quarter >= 2), moved, y_low[t])
            if z == 7 and f < WIND + 2:
                xzbuf[0, pl.ds(f, 1), :] = value[7:8]
                xzbuf[1, pl.ds(f, 1), :] = value[0:1]
    for c in range(4):
        xzbuf[0, pl.ds(10 + c, 1), :] = allf[7][0][c][6:7]
        xzbuf[1, pl.ds(10 + c, 1), :] = allf[7][0][c][1:2]
        xzbuf[0, pl.ds(14 + c, 1), :] = allf[6][1][c][7:8]
        xzbuf[1, pl.ds(14 + c, 1), :] = allf[6][1][c][0:1]
    for side, tiles in ((0, y_high), (1, y_low)):
        xy_high, xy_low = zero, zero
        for t in range(3):
            ybuf[side, t] = tiles[t]
            moved = pltpu.roll(tiles[t], (2 * t + 2) % 8, 0)
            xy_high = jnp.where(row // 2 == t, moved, xy_high)
            xy_low = jnp.where(row // 2 == t + 1, moved, xy_low)
        xybuf[0, side] = xy_high
        xybuf[1, side] = xy_low

    halo = {}

    def post(kind, src, dst, to, dx=0):
        i = sum(len(group) for group in halo.values())
        send_if, recv_if = {0: (None, None), 1: (has_right, has_left), -1: (has_left, has_right)}[dx]
        halo.setdefault(kind, []).append(Sent(src, dst, ss.at[i], rs.at[i], to, send_if, recv_if))

    both = ((0, 1), (1, -1))
    post("z", zbuf, zr, device(0, 0, 1))
    for side, d in both:
        post("xz", xzbuf.at[side], xzr.at[side], device(d, 0, 1), d)
        post("yz", ybuf.at[side, 0], yzr.at[side], device(0, d, 1))
        for x_side, e in both:
            post("xyz", xybuf.at[x_side, side], xyzr.at[x_side, side], device(e, d, 1), e)
    for side, d in both:
        for x_side, e in both:
            post("xy", xybuf.at[x_side, side], xyr.at[x_side, side], device(e, d, 0), e)
        post("y", ybuf.at[side], yr.at[side], device(0, d, 0))
        post("x", xbuf.at[side], xr.at[side], device(d, 0, 0), d)

    @pl.when(has_left & has_right)
    def _():
        pl.semaphore_wait(barrier, 17)

    @pl.when(ix == 0)
    def _():
        pl.semaphore_wait(barrier, 11)
        pl.semaphore_signal(barrier, inc=1, device_id=(nx - 1, iy, iz), device_id_type=MESH)

    @pl.when(ix == nx - 1)
    def _():
        pl.semaphore_wait(barrier, 12)
        pl.semaphore_signal(barrier, inc=1, device_id=(0, iy, iz), device_id_type=MESH)

    for group in halo.values():
        for sent in group:
            sent.start()

    def arrived(*kinds):
        for kind in kinds:
            for sent in halo[kind]:
                sent.wait_recv()

    def add_products(k, base, planes):
        for z in planes:
            zi = plane(z)
            total = get(base, z, OWN) * sav[k, 0, zi]
            for c in range(1, 4):
                total = total + get(base + c, z, OWN) * sav[k, c, zi]
            prod[z] = total if k == 0 else prod[z] + total

    loads[6].wait()
    add_products(0, 0, range(8))

    def masked(f, t, value):
        if f < 4 or WIND <= f < DAMP:
            return jnp.where(inside[t], value, 0.0)
        return value

    def both_y(high, low):
        return jnp.where(quarter < 2, high, low)

    def xy_tile(src, t):
        value = jnp.where(row // 2 == t, both_y(src[0, 0], src[0, 1]), both_y(src[1, 0], src[1, 1]))
        return pltpu.roll(value, (6 - 2 * t) % 8, 0)

    def each(run):
        for z in range(8):
            for f in range(FIELDS):
                run(z, f, (7 - z) * FIELDS + f)

    def unpack_x(z, f, n):
        k = n % 4
        value = jnp.where(row // 2 == k, xr[0, n // 4], xr[1, n // 4])
        put(f, z, XH, masked(f, XH, pltpu.roll(value, (6 - 2 * k) % 8, 0)))

    def unpack_y(z, f, n):
        put(f, z, YH, masked(f, YH, pltpu.roll(y_own[n // 32], (126 - 4 * (n % 32)) % 128, 1)))

    def unpack_xy(z, f, n):
        if f < DAMP:
            put(f, z, XYH, masked(f, XYH, pltpu.roll(xy_own[n // 32], (126 - 4 * (n % 32)) % 128, 1)))

    def unpack_top():
        y_top = both_y(yzr[0], yzr[1])
        xy_top = xy_tile(xyzr, 0)
        for f in range(FIELDS):
            put(f, 8, OWN, zr[f])
            if 4 <= f <= WIND:
                put(f, 9, OWN, zr[FIELDS + f - 4])
            if f < WIND + 2:
                value = jnp.where(row == 7, xzr[0, pl.ds(f, 1), :], xzr[1, pl.ds(f, 1), :])
                put(f, 8, XH, masked(f, XH, value))
            shift = (126 - 4 * f) % 128
            if f < DAMP:
                put(f, 8, YH, masked(f, YH, pltpu.roll(y_top, shift, 1)))
            if f < 4 or WIND <= f < DAMP:
                put(f, 8, XYH, masked(f, XYH, pltpu.roll(xy_top, shift, 1)))
                put(f, 9, YH, masked(f, YH, pltpu.roll(y_top, (126 - 4 * (FIELDS + f)) % 128, 1)))

    def across(own, far, r_up, r_dn, axis):
        size = own.shape[axis]
        up, dn = size - 1, 1
        own_up, own_dn = pltpu.roll(own, up, axis), pltpu.roll(own, dn, axis)
        far_up, far_dn = pltpu.roll(far, up, axis), pltpu.roll(far, dn, axis)
        return (
            jnp.where(r_up, far_up, own_up) - jnp.where(r_dn, far_dn, own_dn),
            jnp.where(r_up, own_up, far_up) - jnp.where(r_dn, own_dn, far_dn),
        )

    def flux_tile(src, z, t):
        return fluxes([get(src + c, z, t) for c in range(4)], [get(WIND + c, z, t) for c in range(3)])

    def flux_plane(src, z, tiles):
        return {t: flux_tile(src, z, t) for t in tiles}

    def seam(flux, r_up, r_dn, axis):
        size = flux.shape[axis]
        return jnp.where(r_up, pltpu.roll(flux, size - 1, axis), 0.0) - jnp.where(r_dn, pltpu.roll(flux, 1, axis), 0.0)

    every, sides = [OWN, XH, YH, XYH], [OWN, XH, YH]
    beside_x = {OWN: XH, XH: OWN, YH: XYH, XYH: YH}
    beside_y = {OWN: YH, YH: OWN, XH: XYH, XYH: XH}

    def first_plane(z):
        if z < 8:
            return flux_plane(0, z, every)
        if z == 8:
            result = flux_plane(0, 8, every)
            fz = result[XH][0]
            for c in range(4):
                lo, hi = xzr[0, pl.ds(10 + c, 1), :], xzr[1, pl.ds(10 + c, 1), :]
                fz[c] = jnp.where(row == 6, lo, jnp.where(row == 1, hi, fz[c]))
            return result
        fx = []
        for c in range(4):
            lo, hi = xzr[0, pl.ds(14 + c, 1), :], xzr[1, pl.ds(14 + c, 1), :]
            fx.append(jnp.where(inside[XH], jnp.where(row == 7, lo, hi), 0.0))
        return {XH: (None, fx, None), YH: flux_tile(0, 9, YH)}

    def first_step(planes):
        held = {}
        for z in planes:
            for w in ([z - 1, z] if z == 8 else [z, z + 1] if z == 7 else [z]):
                if w not in held:
                    held[w] = first_plane(w)
            here = held[z]
            for t in every if z < 8 else sides if z == 8 else [OWN]:
                for c in range(4):
                    sx = seam(here[beside_x[t]][1][c], row7, row0, 0)
                    sy = seam(here[beside_y[t]][2][c], lane127, lane0, 1)
                    value = get(4 + c, z, t) + HALF * (sx + sy)
                    if z == 7:
                        value = value + hz * held[8][t][0][c]
                    if z == 8:
                        value = value - hz * held[7][t][0][c]
                    if t != OWN:
                        value = jnp.where(inside[t], value, 0.0)
                    put(4 + c, z, t, value)

    def step(src, dst, planes, flux_tiles, new_tiles, keep=None):
        held = {}
        for z in planes:
            for w in (z - 1, z, z + 1):
                if w >= 0 and w not in held:
                    held[w] = flux_plane(src, w, flux_tiles[w])
            f = held[z]
            for c in range(4):
                dx, dy = {}, {}
                dx[OWN], dx[XH] = across(f[OWN][1][c], f[XH][1][c], row7, row0, 0)
                dy[OWN], dy[YH] = across(f[OWN][2][c], f[YH][2][c], lane127, lane0, 1)
                if XYH in f:
                    dx[YH], dx[XYH] = across(f[YH][1][c], f[XYH][1][c], row7, row0, 0)
                    dy[XH], dy[XYH] = across(f[XH][2][c], f[XYH][2][c], lane127, lane0, 1)
                for t in new_tiles[z]:
                    dz = held[z + 1][t][0][c]
                    if z > 0:
                        dz = dz - held[z - 1][t][0][c]
                    value = get(dst + c, z, t) + HALF * (dx[t] + dy[t]) + hz * dz - get(DAMP, z, t) * get(src + c, z, t)
                    if t != OWN:
                        value = jnp.where(inside[t], value, 0.0)
                    put(dst + c, z, t, value)
                    if keep is not None:
                        keep(c, z, value)

    def second_step(planes):
        step(4, 0, planes, [every] * 8 + [sides, [OWN]], [sides] * 8 + [[OWN]])

    def keep(c, z, value):
        out[0, c, plane(z)] = value

    def third_step(planes):
        step(0, 4, planes, [sides] * 8 + [[OWN]], [[OWN]] * 8, keep)

    arrived("x")
    each(unpack_x)
    arrived("y")
    y_own = [both_y(yr[0, t], yr[1, t]) for t in range(3)]
    each(unpack_y)
    arrived("xy")
    xy_own = [xy_tile(xyr, t) for t in range(3)]
    each(unpack_xy)
    first_step(range(7))
    add_products(1, 4, range(7))
    second_step(range(6))
    add_products(2, 0, range(6))
    third_step(range(5))
    add_products(3, 4, range(5))

    def slot_sum(s, planes):
        total = zero
        for z in planes:
            total = total + jnp.where(slo[plane(z)] == s + 1, prod[z], 0.0)
        return total

    for s in range(64):
        slots[s] = slot_sum(s, range(5))
    turned = jnp.transpose(jnp.broadcast_to(place[0:1], (128, 128)))[0:64]
    wide = lax.broadcasted_iota(jnp.int32, (64, 128), 1)
    arrived("z", "yz", "xz", "xyz")
    unpack_top()
    first_step(range(7, 10))
    add_products(1, 4, [7])
    second_step(range(6, 9))
    add_products(2, 0, [6, 7])
    third_step(range(5, 8))
    add_products(3, 4, [5, 6, 7])

    for s in range(64):
        total = slots[s] + slot_sum(s, range(5, 8))
        smat[pl.ds(s, 1), :] = jnp.sum(total, axis=0, keepdims=True)
    sums = jnp.sum(smat[...], axis=1, keepdims=True) * (-FULL)
    facades = jnp.sum(jnp.where(turned == wide, sums, 0.0), axis=0, keepdims=True)
    gs[...] = jnp.broadcast_to(facades, (8, 128))

    @pl.when(ix == 0)
    def _():
        pl.semaphore_wait(barrier, 1)

    parts = [
        Sent(gs, gr.at[0], g_ss.at[0], g_rs.at[0], device(1, 0, 0)),
        Sent(gs, gr.at[1], g_ss.at[1], g_rs.at[1], device(-1, 0, 0)),
    ]
    for sent in parts:
        sent.start()

    low, high = zero, zero
    allf = []
    for z in range(8):
        fz, fx, fy = fluxes([get(4 + c, z, OWN) for c in range(4)], [get(WIND + c, z, OWN) for c in range(3)])
        allf.append((fz, fx, fy))
        for c in range(4):
            n = c * 8 + z
            xs[0, pl.ds(n, 1), :] = fx[c][7:8]
            xs[1, pl.ds(n, 1), :] = fx[c][0:1]
            p = 2 * n + 1
            moved = pltpu.roll(fy[c], (p + 1) % 128, 1)
            high = jnp.where(lane == p, moved, high)
            low = jnp.where(lane == (p + 1) % 128, moved, low)
    ys[0], ys[1] = high, low
    for c in range(4):
        zs[c] = allf[7][0][c]
    faces = [
        Sent(ys.at[0], yf.at[0], fs.at[0], fr.at[0], device(0, 1, 0)),
        Sent(ys.at[1], yf.at[1], fs.at[1], fr.at[1], device(0, -1, 0)),
        Sent(zs, zf, fs.at[2], fr.at[2], device(0, 0, 1)),
        Sent(xs.at[0], xf.at[0], fs.at[3], fr.at[3], device(1, 0, 0), has_right, has_left),
        Sent(xs.at[1], xf.at[1], fs.at[4], fr.at[4], device(-1, 0, 0), has_left, has_right),
    ]
    for sent in faces:
        sent.start()
    def hold(c, z, value):
        part[c * 8 + z] = value

    within(lambda c, z: get(4 + c, z, OWN), allf, lambda c, z: get(c, z, OWN), hold)

    for sent in faces:
        sent.wait_recv()
    south = jnp.where(iy > 0, -yf[0], 0.0)
    north = jnp.where(iy < ny - 1, pltpu.roll(yf[1], 126, 1), 0.0)
    rim = HALF * jnp.where(jnp.bitwise_and(lane, 1) == 1, south, north)
    at_left, at_right = row0 & has_left, row7 & has_right
    for z in range(8):
        for c in range(4):
            n = c * 8 + z
            value = part[n]
            edge = pltpu.roll(rim, 128 - (2 * n + 1), 1)
            value = value + jnp.where(lane0 | lane127, edge, 0.0)
            lrow = xf[0, pl.ds(n, 1), :] * (-HALF)
            rrow = xf[1, pl.ds(n, 1), :] * HALF
            value = value + jnp.where(at_left, lrow, jnp.where(at_right, rrow, 0.0))
            if z == 7:
                value = value + hz * zf[c]
            out[1, c, plane(z)] = value
    for sent in parts:
        sent.wait_recv()
    total = gs[...] + pltpu.roll(gr[0], 96, 1) + pltpu.roll(gr[1], 64, 1)
    grad[...] = total[0, 0:FAC_DEV]
    for sent in sum(halo.values(), []) + faces + parts:
        sent.wait_send()


def writer(state, sums, out, grad, sems):
    copies = [pltpu.make_async_copy(sums, grad, sems.at[0])]
    for level in range(2):
        copies.append(pltpu.make_async_copy(state.at[level], out.at[level], sems.at[1 + level]))
    for copy in copies:
        copy.start()
    for copy in copies:
        copy.wait()


def local(sizes, adjoint, saved_state, wind_field, facade_slot, facade_table, impedance):
    imp = impedance.reshape(-1, 128)
    hbm_spec = pl.BlockSpec(memory_space=pltpu.HBM)
    vmem_spec = pl.BlockSpec(memory_space=pltpu.VMEM)
    v = pltpu.VMEM
    dma = pltpu.SemaphoreType.DMA
    steps = saved_state.shape[0]
    assert steps == 4
    state, sums = pl.pallas_call(
        functools.partial(kernel, sizes),
        out_shape=[
            jax.ShapeDtypeStruct(adjoint.shape, F32),
            jax.ShapeDtypeStruct((FAC_DEV,), F32),
        ],
        in_specs=[hbm_spec] * 6,
        out_specs=[vmem_spec, vmem_spec],
        scratch_shapes=[
            v((4, 8, 8, 128), F32),
            v((4, 8, 8, 128), F32),
            v((steps, 4, 8, 8, 128), F32),
            v((3, 8, 8, 128), F32),
            v((8, 8, 128), jnp.int32),
            v((1, 64), jnp.int32),
            v((128, 128), F32),
            v((FIELDS * 10 * 4, 8, 128), F32),
            v((32, 8, 128), F32),
            v((8, 8, 128), F32),
            v((2, 24, 8, 128), F32),
            v((2, 24, 128), F32),
            v((2, 3, 8, 128), F32),
            v((2, 2, 8, 128), F32),
            v((17, 8, 128), F32),
            v((2, 24, 8, 128), F32),
            v((2, 24, 128), F32),
            v((2, 3, 8, 128), F32),
            v((2, 8, 128), F32),
            v((17, 8, 128), F32),
            v((2, 2, 8, 128), F32),
            v((2, 2, 8, 128), F32),
            v((2, 32, 128), F32),
            v((2, 8, 128), F32),
            v((4, 8, 128), F32),
            v((2, 32, 128), F32),
            v((2, 8, 128), F32),
            v((4, 8, 128), F32),
            v((64, 8, 128), F32),
            v((64, 128), F32),
            v((8, 128), F32),
            v((2, 8, 128), F32),
            dma((7,)), dma((17,)), dma((17,)), dma((5,)), dma((5,)), dma((2,)), dma((2,)),
        ],
        compiler_params=pltpu.CompilerParams(
            collective_id=0, has_side_effects=True, vmem_limit_bytes=32 << 20
        ),
    )(*[pltpu.with_memory_space_constraint(a, pltpu.HBM)
        for a in (adjoint, saved_state, wind_field, facade_slot, facade_table, imp)])
    out, grad = pl.pallas_call(
        writer,
        out_shape=[
            jax.ShapeDtypeStruct(adjoint.shape, F32),
            jax.ShapeDtypeStruct((FAC_DEV,), F32),
        ],
        in_specs=[vmem_spec, vmem_spec],
        out_specs=[hbm_spec, hbm_spec],
        scratch_shapes=[dma((3,))],
        compiler_params=pltpu.CompilerParams(vmem_limit_bytes=1 << 20),
    )(state, sums)
    return out, grad


def solution(mesh):
    sizes = tuple(mesh.shape[a] for a in ("gx", "gy", "gz"))
    return jax.shard_map(
        functools.partial(local, sizes),
        mesh=mesh,
        in_specs=(
            P(None, None, "gz", "gx", "gy"),
            P(None, None, "gz", "gx", "gy"),
            P(None, "gz", "gx", "gy"),
            P("gz", "gx", "gy"),
            P("gz", "gx", "gy", None),
            P(),
        ),
        out_specs=(P(None, None, "gz", "gx", "gy"), P(("gx", "gy", "gz"))),
        check_vma=False,
    )
```

```python
import functools

import jax
import jax.numpy as jnp
from jax import lax
from jax.experimental import pallas as pl
from jax.experimental.pallas import tpu as pltpu
from jax.sharding import PartitionSpec as P

FAC_DEV = 32
TIME_STEP = 0.3
HALF = TIME_STEP
FULL = 2.0 * TIME_STEP
MESH = pl.DeviceIdType.MESH
F32 = jnp.float32

WIND, DAMP, FIELDS = 8, 11, 12
OWN, XH, YH, XYH = 0, 1, 2, 3


def when(cond, run):
    if cond is None:
        run()
    else:
        pl.when(cond)(run)


class Sent:
    def __init__(self, src, dst, send_sem, recv_sem, to, send_if=None, recv_if=None):
        self.copy = pltpu.make_async_remote_copy(
            src_ref=src, dst_ref=dst, send_sem=send_sem, recv_sem=recv_sem, device_id=to, device_id_type=MESH
        )
        self.send_if, self.recv_if = send_if, recv_if

    def start(self):
        when(self.send_if, self.copy.start)

    def wait_recv(self):
        when(self.recv_if, self.copy.wait_recv)

    def wait_send(self):
        when(self.send_if, self.copy.wait_send)


def kernel(sizes, adj, saved, wind, slot, table, impedance, out, grad,
           mid, upp, sav, win, slo, tab, imp, ext, part, prod,
           xbuf, xzbuf, ybuf, xybuf, zbuf, xr, xzr, yr, yzr, zr, xyr, xyzr,
           xs, ys, zs, xf, yf, zf, slots, smat, gs, gr,
           in_sem, ss, rs, fs, fr, g_ss, g_rs):
    nx, ny, nz = sizes
    ix, iy, iz = lax.axis_index("gx"), lax.axis_index("gy"), lax.axis_index("gz")
    has_right, has_left = ix < nx - 1, ix > 0

    def device(dx, dy, dz):
        return (
            lax.rem(ix + dx + nx, nx) if dx else ix,
            lax.rem(iy + dy + ny, ny) if dy else iy,
            1 - iz if dz else iz,
        )

    barrier = pltpu.get_barrier_semaphore()
    for dx in (0, 1, -1):
        def greet(dx=dx):
            for dy in (0, 1, -1):
                for dz in (1, 0):
                    if dx or dy or dz:
                        pl.semaphore_signal(barrier, inc=1, device_id=device(dx, dy, dz), device_id_type=MESH)

        when({0: None, 1: has_right, -1: has_left}[dx], greet)

    loads = []
    for i, (src, dst) in enumerate(
        [(table.at[0, 0], tab), (impedance, imp), (slot, slo), (wind, win), (adj.at[1], mid), (adj.at[0], upp), (saved, sav)]
    ):
        copy = pltpu.make_async_copy(src, dst, in_sem.at[i])
        copy.start()
        loads.append(copy)

    lane = lax.broadcasted_iota(jnp.int32, (8, 128), 1)
    row = lax.broadcasted_iota(jnp.int32, (8, 128), 0)
    row0, row7, lane0, lane127 = row == 0, row == 7, lane == 0, lane == 127
    quarter = jnp.bitwise_and(lane, 3)
    x_in = ((row < 4) & has_right) | ((row >= 4) & has_left)
    y_in = ((lane < 64) & (iy < ny - 1)) | ((lane >= 64) & (iy > 0))
    inside = {OWN: None, XH: x_in, YH: y_in, XYH: x_in & y_in}
    flipped = iz == 1
    hz = jnp.where(flipped, -HALF, HALF)

    def plane(z):
        return jnp.where(flipped, 7 - z, z)

    def put(f, z, t, value):
        ext[(f * 10 + z) * 4 + t] = value

    def get(f, z, t):
        return ext[(f * 10 + z) * 4 + t]

    for i in range(3):
        loads[i].wait()
    group = iy * nz + iz
    per_row = 128 // FAC_DEV
    stride = (ny * nz) // per_row
    row_of = [lax.rem(ix + o + nx, nx) * stride + group // per_row for o in (0, 1, -1)]
    ids = jnp.broadcast_to(jnp.concatenate([tab[...], tab[...]], axis=1), (8, 128))
    id_row = lax.shift_right_logical(ids, 7)
    id_lane = jnp.bitwise_and(ids, 127)
    lut = jnp.zeros((8, 128), F32)
    for o in range(3):
        line = jnp.broadcast_to(imp[pl.ds(row_of[o], 1), :], (8, 128))
        lut = jnp.where(id_row == row_of[o], jnp.take_along_axis(line, id_lane, axis=1), lut)
    lut = lut * FULL
    place = jnp.where(id_row == row_of[0], 0, jnp.where(id_row == row_of[1], 32, 64)) + jnp.bitwise_and(ids, 31)
    for z in range(8):
        names = slo[plane(z)]
        value = jnp.take_along_axis(lut, jnp.maximum(names - 1, 0), axis=1)
        put(DAMP, z, OWN, jnp.where(names > 0, value, 0.0))
    for i in range(3, 6):
        loads[i].wait()

    def fluxes(s, w):
        fz = [w[0] * v for v in s]
        fx = [w[1] * v for v in s]
        fy = [w[2] * v for v in s]
        fz[0], fz[1] = fz[0] + s[1], fz[1] + s[0]
        fx[0], fx[2] = fx[0] + s[2], fx[2] + s[0]
        fy[0], fy[3] = fy[0] + s[3], fy[3] + s[0]
        return fz, fx, fy

    zero = jnp.zeros((8, 128), F32)

    def within(level, allf, upper, store):
        for z in range(8):
            d = get(DAMP, z, OWN)
            for c in range(4):
                fz, fx, fy = (allf[z][i][c] for i in range(3))
                dx = jnp.where(row7, 0.0, pltpu.roll(fx, 7, 0)) - jnp.where(row0, 0.0, pltpu.roll(fx, 1, 0))
                dy = jnp.where(lane127, 0.0, pltpu.roll(fy, 127, 1)) - jnp.where(lane0, 0.0, pltpu.roll(fy, 1, 1))
                value = upper(c, z) + HALF * (dx + dy) - d * level(c, z)
                if 0 < z < 7:
                    value = value + hz * (allf[z + 1][0][c] - allf[z - 1][0][c])
                elif z == 0:
                    value = value + hz * allf[1][0][c]
                else:
                    value = value - hz * allf[6][0][c]
                store(c, z, value)

    allf = []
    for z in range(8):
        zi = plane(z)
        own = [mid[c, zi] for c in range(4)]
        wz = [win[c, zi] for c in range(3)]
        for c in range(4):
            put(c, z, OWN, own[c])
        for c in range(3):
            put(WIND + c, z, OWN, wz[c])
        allf.append(fluxes(own, wz))
    within(
        lambda c, z: get(c, z, OWN), allf, lambda c, z: upp[c, plane(z)], lambda c, z, value: put(4 + c, z, OWN, value)
    )

    y_high, y_low = [zero] * 3, [zero] * 3
    for z in reversed(range(8)):
        for f in range(FIELDS):
            value = get(f, z, OWN)
            if z == 7:
                zbuf[f] = value
            if z == 6 and 4 <= f <= WIND:
                zbuf[FIELDS + f - 4] = value
            n = (7 - z) * FIELDS + f
            k = n % 4
            if k == 0:
                x_high = x_low = zero
            moved = pltpu.roll(value, (2 * k + 2) % 8, 0)
            pair, k_next = row // 2, (k + 1) % 4
            x_high = jnp.where(pair == k, moved, x_high)
            x_low = jnp.where(pair == k_next, moved, x_low)
            if k == 3:
                xbuf[0, n // 4] = x_high
                xbuf[1, n // 4] = x_low
            t, k = n // 32, n % 32
            moved = pltpu.roll(value, (4 * k + 2) % 128, 1)
            quad = lane // 4 == k
            y_high[t] = jnp.where(quad & (quarter < 2), moved, y_high[t])
            y_low[t] = jnp.where(quad & (quarter >= 2), moved, y_low[t])
            if z == 7 and f < WIND + 2:
                xzbuf[0, pl.ds(f, 1), :] = value[7:8]
                xzbuf[1, pl.ds(f, 1), :] = value[0:1]
    for c in range(4):
        xzbuf[0, pl.ds(10 + c, 1), :] = allf[7][0][c][6:7]
        xzbuf[1, pl.ds(10 + c, 1), :] = allf[7][0][c][1:2]
        xzbuf[0, pl.ds(14 + c, 1), :] = allf[6][1][c][7:8]
        xzbuf[1, pl.ds(14 + c, 1), :] = allf[6][1][c][0:1]
    for side, tiles in ((0, y_high), (1, y_low)):
        xy_high, xy_low = zero, zero
        for t in range(3):
            ybuf[side, t] = tiles[t]
            moved = pltpu.roll(tiles[t], (2 * t + 2) % 8, 0)
            xy_high = jnp.where(row // 2 == t, moved, xy_high)
            xy_low = jnp.where(row // 2 == t + 1, moved, xy_low)
        xybuf[0, side] = xy_high
        xybuf[1, side] = xy_low

    halo = {}

    def post(kind, src, dst, to, dx=0):
        i = sum(len(group) for group in halo.values())
        send_if, recv_if = {0: (None, None), 1: (has_right, has_left), -1: (has_left, has_right)}[dx]
        halo.setdefault(kind, []).append(Sent(src, dst, ss.at[i], rs.at[i], to, send_if, recv_if))

    both = ((0, 1), (1, -1))
    for side, d in both:
        for x_side, e in both:
            post("xy", xybuf.at[x_side, side], xyr.at[x_side, side], device(e, d, 0), e)
        post("y", ybuf.at[side], yr.at[side], device(0, d, 0))
        post("x", xbuf.at[side], xr.at[side], device(d, 0, 0), d)
    post("z", zbuf, zr, device(0, 0, 1))
    for side, d in both:
        post("xz", xzbuf.at[side], xzr.at[side], device(d, 0, 1), d)
        post("yz", ybuf.at[side, 0], yzr.at[side], device(0, d, 1))
        for x_side, e in both:
            post("xyz", xybuf.at[x_side, side], xyzr.at[x_side, side], device(e, d, 1), e)

    @pl.when(has_left & has_right)
    def _():
        pl.semaphore_wait(barrier, 17)

    @pl.when(ix == 0)
    def _():
        pl.semaphore_wait(barrier, 11)
        pl.semaphore_signal(barrier, inc=1, device_id=(nx - 1, iy, iz), device_id_type=MESH)

    @pl.when(ix == nx - 1)
    def _():
        pl.semaphore_wait(barrier, 12)
        pl.semaphore_signal(barrier, inc=1, device_id=(0, iy, iz), device_id_type=MESH)

    early = lax.rem(ix, 2) == 1
    for kind, group in halo.items():
        for sent in group:
            if kind == "z":
                pl.when(early)(sent.start)
            else:
                sent.start()
    pl.when(jnp.logical_not(early))(halo["z"][0].start)

    def arrived(*kinds):
        for kind in kinds:
            for sent in halo[kind]:
                sent.wait_recv()

    def add_products(k, base, planes):
        for z in planes:
            zi = plane(z)
            total = get(base, z, OWN) * sav[k, 0, zi]
            for c in range(1, 4):
                total = total + get(base + c, z, OWN) * sav[k, c, zi]
            prod[z] = total if k == 0 else prod[z] + total

    loads[6].wait()
    add_products(0, 0, range(8))

    def masked(f, t, value):
        if f < 4 or WIND <= f < DAMP:
            return jnp.where(inside[t], value, 0.0)
        return value

    def both_y(high, low):
        return jnp.where(quarter < 2, high, low)

    def xy_tile(src, t):
        value = jnp.where(row // 2 == t, both_y(src[0, 0], src[0, 1]), both_y(src[1, 0], src[1, 1]))
        return pltpu.roll(value, (6 - 2 * t) % 8, 0)

    def each(run):
        for z in range(8):
            for f in range(FIELDS):
                run(z, f, (7 - z) * FIELDS + f)

    def unpack_x(z, f, n):
        k = n % 4
        value = jnp.where(row // 2 == k, xr[0, n // 4], xr[1, n // 4])
        put(f, z, XH, masked(f, XH, pltpu.roll(value, (6 - 2 * k) % 8, 0)))

    def unpack_y(z, f, n):
        put(f, z, YH, masked(f, YH, pltpu.roll(y_own[n // 32], (126 - 4 * (n % 32)) % 128, 1)))

    def unpack_xy(z, f, n):
        if f < DAMP:
            put(f, z, XYH, masked(f, XYH, pltpu.roll(xy_own[n // 32], (126 - 4 * (n % 32)) % 128, 1)))

    def unpack_top():
        y_top = both_y(yzr[0], yzr[1])
        xy_top = xy_tile(xyzr, 0)
        for f in range(FIELDS):
            put(f, 8, OWN, zr[f])
            if 4 <= f <= WIND:
                put(f, 9, OWN, zr[FIELDS + f - 4])
            if f < WIND + 2:
                value = jnp.where(row == 7, xzr[0, pl.ds(f, 1), :], xzr[1, pl.ds(f, 1), :])
                put(f, 8, XH, masked(f, XH, value))
            shift = (126 - 4 * f) % 128
            if f < DAMP:
                put(f, 8, YH, masked(f, YH, pltpu.roll(y_top, shift, 1)))
            if f < 4 or WIND <= f < DAMP:
                put(f, 8, XYH, masked(f, XYH, pltpu.roll(xy_top, shift, 1)))
                put(f, 9, YH, masked(f, YH, pltpu.roll(y_top, (126 - 4 * (FIELDS + f)) % 128, 1)))

    def across(own, far, r_up, r_dn, axis):
        size = own.shape[axis]
        up, dn = size - 1, 1
        own_up, own_dn = pltpu.roll(own, up, axis), pltpu.roll(own, dn, axis)
        far_up, far_dn = pltpu.roll(far, up, axis), pltpu.roll(far, dn, axis)
        return (
            jnp.where(r_up, far_up, own_up) - jnp.where(r_dn, far_dn, own_dn),
            jnp.where(r_up, own_up, far_up) - jnp.where(r_dn, own_dn, far_dn),
        )

    def flux_tile(src, z, t):
        return fluxes([get(src + c, z, t) for c in range(4)], [get(WIND + c, z, t) for c in range(3)])

    def flux_plane(src, z, tiles):
        return {t: flux_tile(src, z, t) for t in tiles}

    def seam(flux, r_up, r_dn, axis):
        size = flux.shape[axis]
        return jnp.where(r_up, pltpu.roll(flux, size - 1, axis), 0.0) - jnp.where(r_dn, pltpu.roll(flux, 1, axis), 0.0)

    every, sides = [OWN, XH, YH, XYH], [OWN, XH, YH]
    beside_x = {OWN: XH, XH: OWN, YH: XYH, XYH: YH}
    beside_y = {OWN: YH, YH: OWN, XH: XYH, XYH: XH}

    def first_plane(z):
        if z < 8:
            return flux_plane(0, z, every)
        if z == 8:
            result = flux_plane(0, 8, every)
            fz = result[XH][0]
            for c in range(4):
                lo, hi = xzr[0, pl.ds(10 + c, 1), :], xzr[1, pl.ds(10 + c, 1), :]
                fz[c] = jnp.where(row == 6, lo, jnp.where(row == 1, hi, fz[c]))
            return result
        fx = []
        for c in range(4):
            lo, hi = xzr[0, pl.ds(14 + c, 1), :], xzr[1, pl.ds(14 + c, 1), :]
            fx.append(jnp.where(inside[XH], jnp.where(row == 7, lo, hi), 0.0))
        return {XH: (None, fx, None), YH: flux_tile(0, 9, YH)}

    def first_step(planes):
        held = {}
        for z in planes:
            for w in ([z - 1, z] if z == 8 else [z, z + 1] if z == 7 else [z]):
                if w not in held:
                    held[w] = first_plane(w)
            here = held[z]
            for t in every if z < 8 else sides if z == 8 else [OWN]:
                for c in range(4):
                    sx = seam(here[beside_x[t]][1][c], row7, row0, 0)
                    sy = seam(here[beside_y[t]][2][c], lane127, lane0, 1)
                    value = get(4 + c, z, t) + HALF * (sx + sy)
                    if z == 7:
                        value = value + hz * held[8][t][0][c]
                    if z == 8:
                        value = value - hz * held[7][t][0][c]
                    if t != OWN:
                        value = jnp.where(inside[t], value, 0.0)
                    put(4 + c, z, t, value)

    def step(src, dst, planes, flux_tiles, new_tiles, keep=None):
        held = {}
        for z in planes:
            for w in (z - 1, z, z + 1):
                if w >= 0 and w not in held:
                    held[w] = flux_plane(src, w, flux_tiles[w])
            f = held[z]
            for c in range(4):
                dx, dy = {}, {}
                dx[OWN], dx[XH] = across(f[OWN][1][c], f[XH][1][c], row7, row0, 0)
                dy[OWN], dy[YH] = across(f[OWN][2][c], f[YH][2][c], lane127, lane0, 1)
                if XYH in f:
                    dx[YH], dx[XYH] = across(f[YH][1][c], f[XYH][1][c], row7, row0, 0)
                    dy[XH], dy[XYH] = across(f[XH][2][c], f[XYH][2][c], lane127, lane0, 1)
                for t in new_tiles[z]:
                    dz = held[z + 1][t][0][c]
                    if z > 0:
                        dz = dz - held[z - 1][t][0][c]
                    value = get(dst + c, z, t) + HALF * (dx[t] + dy[t]) + hz * dz - get(DAMP, z, t) * get(src + c, z, t)
                    if t != OWN:
                        value = jnp.where(inside[t], value, 0.0)
                    put(dst + c, z, t, value)
                    if keep is not None:
                        keep(c, z, value)

    def second_step(planes):
        step(4, 0, planes, [every] * 8 + [sides, [OWN]], [sides] * 8 + [[OWN]])

    def keep(c, z, value):
        out[0, c, plane(z)] = value

    def third_step(planes):
        step(0, 4, planes, [sides] * 8 + [[OWN]], [[OWN]] * 8, keep)

    arrived("x")
    each(unpack_x)
    arrived("y")
    y_own = [both_y(yr[0, t], yr[1, t]) for t in range(3)]
    each(unpack_y)
    arrived("xy")
    xy_own = [xy_tile(xyr, t) for t in range(3)]
    each(unpack_xy)
    first_step(range(7))
    add_products(1, 4, range(7))
    second_step(range(6))
    add_products(2, 0, range(6))
    third_step(range(5))
    add_products(3, 4, range(5))

    def slot_sum(s, planes):
        total = zero
        for z in planes:
            total = total + jnp.where(slo[plane(z)] == s + 1, prod[z], 0.0)
        return total

    for s in range(64):
        slots[s] = slot_sum(s, range(5))
    turned = jnp.transpose(jnp.broadcast_to(place[0:1], (128, 128)))[0:64]
    wide = lax.broadcasted_iota(jnp.int32, (64, 128), 1)
    arrived("z", "yz", "xz", "xyz")
    unpack_top()
    first_step(range(7, 10))
    add_products(1, 4, [7])
    second_step(range(6, 9))
    add_products(2, 0, [6, 7])
    third_step(range(5, 8))
    add_products(3, 4, [5, 6, 7])

    for s in range(64):
        total = slots[s] + slot_sum(s, range(5, 8))
        smat[pl.ds(s, 1), :] = jnp.sum(total, axis=0, keepdims=True)
    sums = jnp.sum(smat[...], axis=1, keepdims=True) * (-FULL)
    facades = jnp.sum(jnp.where(turned == wide, sums, 0.0), axis=0, keepdims=True)
    gs[...] = jnp.broadcast_to(facades, (8, 128))

    @pl.when(ix == 0)
    def _():
        pl.semaphore_wait(barrier, 1)

    parts = [
        Sent(gs, gr.at[0], g_ss.at[0], g_rs.at[0], device(1, 0, 0)),
        Sent(gs, gr.at[1], g_ss.at[1], g_rs.at[1], device(-1, 0, 0)),
    ]
    for sent in parts:
        sent.start()

    low, high = zero, zero
    allf = []
    for z in range(8):
        fz, fx, fy = fluxes([get(4 + c, z, OWN) for c in range(4)], [get(WIND + c, z, OWN) for c in range(3)])
        allf.append((fz, fx, fy))
        for c in range(4):
            n = c * 8 + z
            xs[0, pl.ds(n, 1), :] = fx[c][7:8]
            xs[1, pl.ds(n, 1), :] = fx[c][0:1]
            p = 2 * n + 1
            moved = pltpu.roll(fy[c], (p + 1) % 128, 1)
            high = jnp.where(lane == p, moved, high)
            low = jnp.where(lane == (p + 1) % 128, moved, low)
    ys[0], ys[1] = high, low
    for c in range(4):
        zs[c] = allf[7][0][c]
    faces = [
        Sent(ys.at[0], yf.at[0], fs.at[0], fr.at[0], device(0, 1, 0)),
        Sent(ys.at[1], yf.at[1], fs.at[1], fr.at[1], device(0, -1, 0)),
        Sent(zs, zf, fs.at[2], fr.at[2], device(0, 0, 1)),
        Sent(xs.at[0], xf.at[0], fs.at[3], fr.at[3], device(1, 0, 0), has_right, has_left),
        Sent(xs.at[1], xf.at[1], fs.at[4], fr.at[4], device(-1, 0, 0), has_left, has_right),
    ]
    for sent in faces:
        sent.start()
    def hold(c, z, value):
        part[c * 8 + z] = value

    within(lambda c, z: get(4 + c, z, OWN), allf, lambda c, z: get(c, z, OWN), hold)

    for sent in faces:
        sent.wait_recv()
    south = jnp.where(iy > 0, -yf[0], 0.0)
    north = jnp.where(iy < ny - 1, pltpu.roll(yf[1], 126, 1), 0.0)
    rim = HALF * jnp.where(jnp.bitwise_and(lane, 1) == 1, south, north)
    at_left, at_right = row0 & has_left, row7 & has_right
    for z in range(8):
        for c in range(4):
            n = c * 8 + z
            value = part[n]
            edge = pltpu.roll(rim, 128 - (2 * n + 1), 1)
            value = value + jnp.where(lane0 | lane127, edge, 0.0)
            lrow = xf[0, pl.ds(n, 1), :] * (-HALF)
            rrow = xf[1, pl.ds(n, 1), :] * HALF
            value = value + jnp.where(at_left, lrow, jnp.where(at_right, rrow, 0.0))
            if z == 7:
                value = value + hz * zf[c]
            out[1, c, plane(z)] = value
    for sent in parts:
        sent.wait_recv()
    total = gs[...] + pltpu.roll(gr[0], 96, 1) + pltpu.roll(gr[1], 64, 1)
    grad[...] = total[0, 0:FAC_DEV]
    for sent in sum(halo.values(), []) + faces + parts:
        sent.wait_send()


def writer(state, sums, out, grad, sems):
    copies = [pltpu.make_async_copy(sums, grad, sems.at[0])]
    for level in range(2):
        copies.append(pltpu.make_async_copy(state.at[level], out.at[level], sems.at[1 + level]))
    for copy in copies:
        copy.start()
    for copy in copies:
        copy.wait()


def local(sizes, adjoint, saved_state, wind_field, facade_slot, facade_table, impedance):
    imp = impedance.reshape(-1, 128)
    hbm_spec = pl.BlockSpec(memory_space=pltpu.HBM)
    vmem_spec = pl.BlockSpec(memory_space=pltpu.VMEM)
    v = pltpu.VMEM
    dma = pltpu.SemaphoreType.DMA
    steps = saved_state.shape[0]
    assert steps == 4
    state, sums = pl.pallas_call(
        functools.partial(kernel, sizes),
        out_shape=[
            jax.ShapeDtypeStruct(adjoint.shape, F32),
            jax.ShapeDtypeStruct((FAC_DEV,), F32),
        ],
        in_specs=[hbm_spec] * 6,
        out_specs=[vmem_spec, vmem_spec],
        scratch_shapes=[
            v((4, 8, 8, 128), F32),
            v((4, 8, 8, 128), F32),
            v((steps, 4, 8, 8, 128), F32),
            v((3, 8, 8, 128), F32),
            v((8, 8, 128), jnp.int32),
            v((1, 64), jnp.int32),
            v((128, 128), F32),
            v((FIELDS * 10 * 4, 8, 128), F32),
            v((32, 8, 128), F32),
            v((8, 8, 128), F32),
            v((2, 24, 8, 128), F32),
            v((2, 24, 128), F32),
            v((2, 3, 8, 128), F32),
            v((2, 2, 8, 128), F32),
            v((17, 8, 128), F32),
            v((2, 24, 8, 128), F32),
            v((2, 24, 128), F32),
            v((2, 3, 8, 128), F32),
            v((2, 8, 128), F32),
            v((17, 8, 128), F32),
            v((2, 2, 8, 128), F32),
            v((2, 2, 8, 128), F32),
            v((2, 32, 128), F32),
            v((2, 8, 128), F32),
            v((4, 8, 128), F32),
            v((2, 32, 128), F32),
            v((2, 8, 128), F32),
            v((4, 8, 128), F32),
            v((64, 8, 128), F32),
            v((64, 128), F32),
            v((8, 128), F32),
            v((2, 8, 128), F32),
            dma((7,)), dma((17,)), dma((17,)), dma((5,)), dma((5,)), dma((2,)), dma((2,)),
        ],
        compiler_params=pltpu.CompilerParams(
            collective_id=0, has_side_effects=True, vmem_limit_bytes=32 << 20
        ),
    )(*[pltpu.with_memory_space_constraint(a, pltpu.HBM)
        for a in (adjoint, saved_state, wind_field, facade_slot, facade_table, imp)])
    out, grad = pl.pallas_call(
        writer,
        out_shape=[
            jax.ShapeDtypeStruct(adjoint.shape, F32),
            jax.ShapeDtypeStruct((FAC_DEV,), F32),
        ],
        in_specs=[vmem_spec, vmem_spec],
        out_specs=[hbm_spec, hbm_spec],
        scratch_shapes=[dma((3,))],
        compiler_params=pltpu.CompilerParams(vmem_limit_bytes=1 << 20),
    )(state, sums)
    return out, grad


def solution(mesh):
    sizes = tuple(mesh.shape[a] for a in ("gx", "gy", "gz"))
    return jax.shard_map(
        functools.partial(local, sizes),
        mesh=mesh,
        in_specs=(
            P(None, None, "gz", "gx", "gy"),
            P(None, None, "gz", "gx", "gy"),
            P(None, "gz", "gx", "gy"),
            P("gz", "gx", "gy"),
            P("gz", "gx", "gy", None),
            P(),
        ),
        out_specs=(P(None, None, "gz", "gx", "gy"), P(("gx", "gy", "gz"))),
        check_vma=False,
    )
```

```python
import functools

import jax
import jax.numpy as jnp
from jax import lax
from jax.experimental import pallas as pl
from jax.experimental.pallas import tpu as pltpu
from jax.sharding import PartitionSpec as P

FAC_DEV = 32
TIME_STEP = 0.3
HALF = TIME_STEP
FULL = 2.0 * TIME_STEP
MESH = pl.DeviceIdType.MESH
F32 = jnp.float32

WIND, DAMP, FIELDS = 8, 11, 12
OWN, XH, YH, XYH = 0, 1, 2, 3


def when(cond, run):
    if cond is None:
        run()
    else:
        pl.when(cond)(run)


class Sent:
    def __init__(self, src, dst, send_sem, recv_sem, to, send_if=None, recv_if=None):
        self.copy = pltpu.make_async_remote_copy(
            src_ref=src, dst_ref=dst, send_sem=send_sem, recv_sem=recv_sem, device_id=to, device_id_type=MESH
        )
        self.send_if, self.recv_if = send_if, recv_if

    def start(self):
        when(self.send_if, self.copy.start)

    def wait_recv(self):
        when(self.recv_if, self.copy.wait_recv)

    def wait_send(self):
        when(self.send_if, self.copy.wait_send)


def kernel(sizes, adj, saved, wind, slot, table, impedance, out, grad,
           mid, upp, sav, win, slo, tab, imp, ext, part, prod,
           xbuf, xzbuf, ybuf, xybuf, zbuf, xr, xzr, yr, yzr, zr, xyr, xyzr,
           xs, ys, zs, xf, yf, zf, slots, smat, gs, gr,
           in_sem, ss, rs, fs, fr, g_ss, g_rs):
    nx, ny, nz = sizes
    ix, iy, iz = lax.axis_index("gx"), lax.axis_index("gy"), lax.axis_index("gz")
    has_right, has_left = ix < nx - 1, ix > 0

    def device(dx, dy, dz):
        return (
            lax.rem(ix + dx + nx, nx) if dx else ix,
            lax.rem(iy + dy + ny, ny) if dy else iy,
            1 - iz if dz else iz,
        )

    barrier = pltpu.get_barrier_semaphore()
    for dx in (0, 1, -1):
        def greet(dx=dx):
            for dy in (0, 1, -1):
                for dz in (1, 0):
                    if dx or dy or dz:
                        pl.semaphore_signal(barrier, inc=1, device_id=device(dx, dy, dz), device_id_type=MESH)

        when({0: None, 1: has_right, -1: has_left}[dx], greet)

    loads = []
    for i, (src, dst) in enumerate(
        [(table.at[0, 0], tab), (impedance, imp), (slot, slo), (wind, win), (adj.at[1], mid), (adj.at[0], upp), (saved, sav)]
    ):
        copy = pltpu.make_async_copy(src, dst, in_sem.at[i])
        copy.start()
        loads.append(copy)

    lane = lax.broadcasted_iota(jnp.int32, (8, 128), 1)
    row = lax.broadcasted_iota(jnp.int32, (8, 128), 0)
    row0, row7, lane0, lane127 = row == 0, row == 7, lane == 0, lane == 127
    quarter = jnp.bitwise_and(lane, 3)
    x_in = ((row < 4) & has_right) | ((row >= 4) & has_left)
    y_in = ((lane < 64) & (iy < ny - 1)) | ((lane >= 64) & (iy > 0))
    inside = {OWN: None, XH: x_in, YH: y_in, XYH: x_in & y_in}
    flipped = iz == 1
    hz = jnp.where(flipped, -HALF, HALF)

    def plane(z):
        return jnp.where(flipped, 7 - z, z)

    def put(f, z, t, value):
        ext[(f * 10 + z) * 4 + t] = value

    def get(f, z, t):
        return ext[(f * 10 + z) * 4 + t]

    for i in range(3):
        loads[i].wait()
    group = iy * nz + iz
    per_row = 128 // FAC_DEV
    stride = (ny * nz) // per_row
    row_of = [lax.rem(ix + o + nx, nx) * stride + group // per_row for o in (0, 1, -1)]
    ids = jnp.broadcast_to(jnp.concatenate([tab[...], tab[...]], axis=1), (8, 128))
    id_row = lax.shift_right_logical(ids, 7)
    id_lane = jnp.bitwise_and(ids, 127)
    lut = jnp.zeros((8, 128), F32)
    for o in range(3):
        line = jnp.broadcast_to(imp[pl.ds(row_of[o], 1), :], (8, 128))
        lut = jnp.where(id_row == row_of[o], jnp.take_along_axis(line, id_lane, axis=1), lut)
    lut = lut * FULL
    place = jnp.where(id_row == row_of[0], 0, jnp.where(id_row == row_of[1], 32, 64)) + jnp.bitwise_and(ids, 31)
    for z in range(8):
        names = slo[plane(z)]
        value = jnp.take_along_axis(lut, jnp.maximum(names - 1, 0), axis=1)
        put(DAMP, z, OWN, jnp.where(names > 0, value, 0.0))
    for i in range(3, 6):
        loads[i].wait()

    def fluxes(s, w):
        fz = [w[0] * v for v in s]
        fx = [w[1] * v for v in s]
        fy = [w[2] * v for v in s]
        fz[0], fz[1] = fz[0] + s[1], fz[1] + s[0]
        fx[0], fx[2] = fx[0] + s[2], fx[2] + s[0]
        fy[0], fy[3] = fy[0] + s[3], fy[3] + s[0]
        return fz, fx, fy

    zero = jnp.zeros((8, 128), F32)

    def within(level, allf, upper, store):
        for z in range(8):
            d = get(DAMP, z, OWN)
            for c in range(4):
                fz, fx, fy = (allf[z][i][c] for i in range(3))
                dx = jnp.where(row7, 0.0, pltpu.roll(fx, 7, 0)) - jnp.where(row0, 0.0, pltpu.roll(fx, 1, 0))
                dy = jnp.where(lane127, 0.0, pltpu.roll(fy, 127, 1)) - jnp.where(lane0, 0.0, pltpu.roll(fy, 1, 1))
                value = upper(c, z) + HALF * (dx + dy) - d * level(c, z)
                if 0 < z < 7:
                    value = value + hz * (allf[z + 1][0][c] - allf[z - 1][0][c])
                elif z == 0:
                    value = value + hz * allf[1][0][c]
                else:
                    value = value - hz * allf[6][0][c]
                store(c, z, value)

    allf = []
    for z in range(8):
        zi = plane(z)
        own = [mid[c, zi] for c in range(4)]
        wz = [win[c, zi] for c in range(3)]
        for c in range(4):
            put(c, z, OWN, own[c])
        for c in range(3):
            put(WIND + c, z, OWN, wz[c])
        allf.append(fluxes(own, wz))
    within(
        lambda c, z: get(c, z, OWN), allf, lambda c, z: upp[c, plane(z)], lambda c, z, value: put(4 + c, z, OWN, value)
    )

    y_high, y_low = [zero] * 3, [zero] * 3
    for z in reversed(range(8)):
        for f in range(FIELDS):
            value = get(f, z, OWN)
            if z == 7:
                zbuf[f] = value
            if z == 6 and 4 <= f <= WIND:
                zbuf[FIELDS + f - 4] = value
            n = (7 - z) * FIELDS + f
            k = n % 4
            if k == 0:
                x_high = x_low = zero
            moved = pltpu.roll(value, (2 * k + 2) % 8, 0)
            pair, k_next = row // 2, (k + 1) % 4
            x_high = jnp.where(pair == k, moved, x_high)
            x_low = jnp.where(pair == k_next, moved, x_low)
            if k == 3:
                xbuf[0, n // 4] = x_high
                xbuf[1, n // 4] = x_low
            t, k = n // 32, n % 32
            moved = pltpu.roll(value, (4 * k + 2) % 128, 1)
            quad = lane // 4 == k
            y_high[t] = jnp.where(quad & (quarter < 2), moved, y_high[t])
            y_low[t] = jnp.where(quad & (quarter >= 2), moved, y_low[t])
            if z == 7 and f < WIND + 2:
                xzbuf[0, pl.ds(f, 1), :] = value[7:8]
                xzbuf[1, pl.ds(f, 1), :] = value[0:1]
    for c in range(4):
        xzbuf[0, pl.ds(10 + c, 1), :] = allf[7][0][c][6:7]
        xzbuf[1, pl.ds(10 + c, 1), :] = allf[7][0][c][1:2]
        xzbuf[0, pl.ds(14 + c, 1), :] = allf[6][1][c][7:8]
        xzbuf[1, pl.ds(14 + c, 1), :] = allf[6][1][c][0:1]
    for side, tiles in ((0, y_high), (1, y_low)):
        xy_high, xy_low = zero, zero
        for t in range(3):
            ybuf[side, t] = tiles[t]
            moved = pltpu.roll(tiles[t], (2 * t + 2) % 8, 0)
            xy_high = jnp.where(row // 2 == t, moved, xy_high)
            xy_low = jnp.where(row // 2 == t + 1, moved, xy_low)
        xybuf[0, side] = xy_high
        xybuf[1, side] = xy_low

    halo = {}

    def post(kind, src, dst, to, dx=0):
        i = sum(len(group) for group in halo.values())
        send_if, recv_if = {0: (None, None), 1: (has_right, has_left), -1: (has_left, has_right)}[dx]
        halo.setdefault(kind, []).append(Sent(src, dst, ss.at[i], rs.at[i], to, send_if, recv_if))

    both = ((0, 1), (1, -1))
    for side, d in both:
        for x_side, e in both:
            post("xy", xybuf.at[x_side, side], xyr.at[x_side, side], device(e, d, 0), e)
        post("y", ybuf.at[side], yr.at[side], device(0, d, 0))
        post("x", xbuf.at[side], xr.at[side], device(d, 0, 0), d)
    post("z", zbuf, zr, device(0, 0, 1))
    for side, d in both:
        post("xz", xzbuf.at[side], xzr.at[side], device(d, 0, 1), d)
        post("yz", ybuf.at[side, 0], yzr.at[side], device(0, d, 1))
        for x_side, e in both:
            post("xyz", xybuf.at[x_side, side], xyzr.at[x_side, side], device(e, d, 1), e)

    @pl.when(has_left & has_right)
    def _():
        pl.semaphore_wait(barrier, 17)

    @pl.when(ix == 0)
    def _():
        pl.semaphore_wait(barrier, 11)
        pl.semaphore_signal(barrier, inc=1, device_id=(nx - 1, iy, iz), device_id_type=MESH)

    @pl.when(ix == nx - 1)
    def _():
        pl.semaphore_wait(barrier, 12)
        pl.semaphore_signal(barrier, inc=1, device_id=(0, iy, iz), device_id_type=MESH)

    odd = lax.rem(ix, 2) == 1

    def start(*kinds):
        for kind in kinds:
            for sent in halo[kind]:
                sent.start()

    pl.when(odd)(lambda: start("y", "yz", "z", "x", "xy", "xz", "xyz"))
    pl.when(jnp.logical_not(odd))(lambda: start("x", "xy", "xz", "xyz", "y", "yz", "z"))

    def arrived(*kinds):
        for kind in kinds:
            for sent in halo[kind]:
                sent.wait_recv()

    def add_products(k, base, planes):
        for z in planes:
            zi = plane(z)
            total = get(base, z, OWN) * sav[k, 0, zi]
            for c in range(1, 4):
                total = total + get(base + c, z, OWN) * sav[k, c, zi]
            prod[z] = total if k == 0 else prod[z] + total

    loads[6].wait()
    add_products(0, 0, range(8))

    def masked(f, t, value):
        if f < 4 or WIND <= f < DAMP:
            return jnp.where(inside[t], value, 0.0)
        return value

    def both_y(high, low):
        return jnp.where(quarter < 2, high, low)

    def xy_tile(src, t):
        value = jnp.where(row // 2 == t, both_y(src[0, 0], src[0, 1]), both_y(src[1, 0], src[1, 1]))
        return pltpu.roll(value, (6 - 2 * t) % 8, 0)

    def each(run):
        for z in range(8):
            for f in range(FIELDS):
                run(z, f, (7 - z) * FIELDS + f)

    def unpack_x(z, f, n):
        k = n % 4
        value = jnp.where(row // 2 == k, xr[0, n // 4], xr[1, n // 4])
        put(f, z, XH, masked(f, XH, pltpu.roll(value, (6 - 2 * k) % 8, 0)))

    def unpack_y(z, f, n):
        put(f, z, YH, masked(f, YH, pltpu.roll(y_own[n // 32], (126 - 4 * (n % 32)) % 128, 1)))

    def unpack_xy(z, f, n):
        if f < DAMP:
            put(f, z, XYH, masked(f, XYH, pltpu.roll(xy_own[n // 32], (126 - 4 * (n % 32)) % 128, 1)))

    def unpack_top():
        y_top = both_y(yzr[0], yzr[1])
        xy_top = xy_tile(xyzr, 0)
        for f in range(FIELDS):
            put(f, 8, OWN, zr[f])
            if 4 <= f <= WIND:
                put(f, 9, OWN, zr[FIELDS + f - 4])
            if f < WIND + 2:
                value = jnp.where(row == 7, xzr[0, pl.ds(f, 1), :], xzr[1, pl.ds(f, 1), :])
                put(f, 8, XH, masked(f, XH, value))
            shift = (126 - 4 * f) % 128
            if f < DAMP:
                put(f, 8, YH, masked(f, YH, pltpu.roll(y_top, shift, 1)))
            if f < 4 or WIND <= f < DAMP:
                put(f, 8, XYH, masked(f, XYH, pltpu.roll(xy_top, shift, 1)))
                put(f, 9, YH, masked(f, YH, pltpu.roll(y_top, (126 - 4 * (FIELDS + f)) % 128, 1)))

    def across(own, far, r_up, r_dn, axis):
        size = own.shape[axis]
        up, dn = size - 1, 1
        own_up, own_dn = pltpu.roll(own, up, axis), pltpu.roll(own, dn, axis)
        far_up, far_dn = pltpu.roll(far, up, axis), pltpu.roll(far, dn, axis)
        return (
            jnp.where(r_up, far_up, own_up) - jnp.where(r_dn, far_dn, own_dn),
            jnp.where(r_up, own_up, far_up) - jnp.where(r_dn, own_dn, far_dn),
        )

    def flux_tile(src, z, t):
        return fluxes([get(src + c, z, t) for c in range(4)], [get(WIND + c, z, t) for c in range(3)])

    def flux_plane(src, z, tiles):
        return {t: flux_tile(src, z, t) for t in tiles}

    def seam(flux, r_up, r_dn, axis):
        size = flux.shape[axis]
        return jnp.where(r_up, pltpu.roll(flux, size - 1, axis), 0.0) - jnp.where(r_dn, pltpu.roll(flux, 1, axis), 0.0)

    every, sides = [OWN, XH, YH, XYH], [OWN, XH, YH]
    beside_x = {OWN: XH, XH: OWN, YH: XYH, XYH: YH}
    beside_y = {OWN: YH, YH: OWN, XH: XYH, XYH: XH}

    def first_plane(z):
        if z < 8:
            return flux_plane(0, z, every)
        if z == 8:
            result = flux_plane(0, 8, every)
            fz = result[XH][0]
            for c in range(4):
                lo, hi = xzr[0, pl.ds(10 + c, 1), :], xzr[1, pl.ds(10 + c, 1), :]
                fz[c] = jnp.where(row == 6, lo, jnp.where(row == 1, hi, fz[c]))
            return result
        fx = []
        for c in range(4):
            lo, hi = xzr[0, pl.ds(14 + c, 1), :], xzr[1, pl.ds(14 + c, 1), :]
            fx.append(jnp.where(inside[XH], jnp.where(row == 7, lo, hi), 0.0))
        return {XH: (None, fx, None), YH: flux_tile(0, 9, YH)}

    def first_step(planes):
        held = {}
        for z in planes:
            for w in ([z - 1, z] if z == 8 else [z, z + 1] if z == 7 else [z]):
                if w not in held:
                    held[w] = first_plane(w)
            here = held[z]
            for t in every if z < 8 else sides if z == 8 else [OWN]:
                for c in range(4):
                    sx = seam(here[beside_x[t]][1][c], row7, row0, 0)
                    sy = seam(here[beside_y[t]][2][c], lane127, lane0, 1)
                    value = get(4 + c, z, t) + HALF * (sx + sy)
                    if z == 7:
                        value = value + hz * held[8][t][0][c]
                    if z == 8:
                        value = value - hz * held[7][t][0][c]
                    if t != OWN:
                        value = jnp.where(inside[t], value, 0.0)
                    put(4 + c, z, t, value)

    def step(src, dst, planes, flux_tiles, new_tiles, keep=None):
        held = {}
        for z in planes:
            for w in (z - 1, z, z + 1):
                if w >= 0 and w not in held:
                    held[w] = flux_plane(src, w, flux_tiles[w])
            f = held[z]
            for c in range(4):
                dx, dy = {}, {}
                dx[OWN], dx[XH] = across(f[OWN][1][c], f[XH][1][c], row7, row0, 0)
                dy[OWN], dy[YH] = across(f[OWN][2][c], f[YH][2][c], lane127, lane0, 1)
                if XYH in f:
                    dx[YH], dx[XYH] = across(f[YH][1][c], f[XYH][1][c], row7, row0, 0)
                    dy[XH], dy[XYH] = across(f[XH][2][c], f[XYH][2][c], lane127, lane0, 1)
                for t in new_tiles[z]:
                    dz = held[z + 1][t][0][c]
                    if z > 0:
                        dz = dz - held[z - 1][t][0][c]
                    value = get(dst + c, z, t) + HALF * (dx[t] + dy[t]) + hz * dz - get(DAMP, z, t) * get(src + c, z, t)
                    if t != OWN:
                        value = jnp.where(inside[t], value, 0.0)
                    put(dst + c, z, t, value)
                    if keep is not None:
                        keep(c, z, value)

    def second_step(planes):
        step(4, 0, planes, [every] * 8 + [sides, [OWN]], [sides] * 8 + [[OWN]])

    def keep(c, z, value):
        out[0, c, plane(z)] = value

    def third_step(planes):
        step(0, 4, planes, [sides] * 8 + [[OWN]], [[OWN]] * 8, keep)

    arrived("x")
    each(unpack_x)
    arrived("y")
    y_own = [both_y(yr[0, t], yr[1, t]) for t in range(3)]
    each(unpack_y)
    arrived("xy")
    xy_own = [xy_tile(xyr, t) for t in range(3)]
    each(unpack_xy)
    first_step(range(7))
    add_products(1, 4, range(7))
    second_step(range(6))
    add_products(2, 0, range(6))
    third_step(range(5))
    add_products(3, 4, range(5))

    def slot_sum(s, planes):
        total = zero
        for z in planes:
            total = total + jnp.where(slo[plane(z)] == s + 1, prod[z], 0.0)
        return total

    for s in range(64):
        slots[s] = slot_sum(s, range(5))
    turned = jnp.transpose(jnp.broadcast_to(place[0:1], (128, 128)))[0:64]
    wide = lax.broadcasted_iota(jnp.int32, (64, 128), 1)
    arrived("z", "yz", "xz", "xyz")
    unpack_top()
    first_step(range(7, 10))
    add_products(1, 4, [7])
    second_step(range(6, 9))
    add_products(2, 0, [6, 7])
    third_step(range(5, 8))
    add_products(3, 4, [5, 6, 7])

    for s in range(64):
        total = slots[s] + slot_sum(s, range(5, 8))
        smat[pl.ds(s, 1), :] = jnp.sum(total, axis=0, keepdims=True)
    sums = jnp.sum(smat[...], axis=1, keepdims=True) * (-FULL)
    facades = jnp.sum(jnp.where(turned == wide, sums, 0.0), axis=0, keepdims=True)
    gs[...] = jnp.broadcast_to(facades, (8, 128))

    @pl.when(ix == 0)
    def _():
        pl.semaphore_wait(barrier, 1)

    parts = [
        Sent(gs, gr.at[0], g_ss.at[0], g_rs.at[0], device(1, 0, 0)),
        Sent(gs, gr.at[1], g_ss.at[1], g_rs.at[1], device(-1, 0, 0)),
    ]
    for sent in parts:
        sent.start()

    low, high = zero, zero
    allf = []
    for z in range(8):
        fz, fx, fy = fluxes([get(4 + c, z, OWN) for c in range(4)], [get(WIND + c, z, OWN) for c in range(3)])
        allf.append((fz, fx, fy))
        for c in range(4):
            n = c * 8 + z
            xs[0, pl.ds(n, 1), :] = fx[c][7:8]
            xs[1, pl.ds(n, 1), :] = fx[c][0:1]
            p = 2 * n + 1
            moved = pltpu.roll(fy[c], (p + 1) % 128, 1)
            high = jnp.where(lane == p, moved, high)
            low = jnp.where(lane == (p + 1) % 128, moved, low)
    ys[0], ys[1] = high, low
    for c in range(4):
        zs[c] = allf[7][0][c]
    faces = [
        Sent(ys.at[0], yf.at[0], fs.at[0], fr.at[0], device(0, 1, 0)),
        Sent(ys.at[1], yf.at[1], fs.at[1], fr.at[1], device(0, -1, 0)),
        Sent(zs, zf, fs.at[2], fr.at[2], device(0, 0, 1)),
        Sent(xs.at[0], xf.at[0], fs.at[3], fr.at[3], device(1, 0, 0), has_right, has_left),
        Sent(xs.at[1], xf.at[1], fs.at[4], fr.at[4], device(-1, 0, 0), has_left, has_right),
    ]
    for sent in faces:
        sent.start()
    def hold(c, z, value):
        part[c * 8 + z] = value

    within(lambda c, z: get(4 + c, z, OWN), allf, lambda c, z: get(c, z, OWN), hold)

    for sent in faces:
        sent.wait_recv()
    south = jnp.where(iy > 0, -yf[0], 0.0)
    north = jnp.where(iy < ny - 1, pltpu.roll(yf[1], 126, 1), 0.0)
    rim = HALF * jnp.where(jnp.bitwise_and(lane, 1) == 1, south, north)
    at_left, at_right = row0 & has_left, row7 & has_right
    for z in range(8):
        for c in range(4):
            n = c * 8 + z
            value = part[n]
            edge = pltpu.roll(rim, 128 - (2 * n + 1), 1)
            value = value + jnp.where(lane0 | lane127, edge, 0.0)
            lrow = xf[0, pl.ds(n, 1), :] * (-HALF)
            rrow = xf[1, pl.ds(n, 1), :] * HALF
            value = value + jnp.where(at_left, lrow, jnp.where(at_right, rrow, 0.0))
            if z == 7:
                value = value + hz * zf[c]
            out[1, c, plane(z)] = value
    for sent in parts:
        sent.wait_recv()
    total = gs[...] + pltpu.roll(gr[0], 96, 1) + pltpu.roll(gr[1], 64, 1)
    grad[...] = total[0, 0:FAC_DEV]
    for sent in sum(halo.values(), []) + faces + parts:
        sent.wait_send()


def writer(state, sums, out, grad, sems):
    copies = [pltpu.make_async_copy(sums, grad, sems.at[0])]
    for level in range(2):
        copies.append(pltpu.make_async_copy(state.at[level], out.at[level], sems.at[1 + level]))
    for copy in copies:
        copy.start()
    for copy in copies:
        copy.wait()


def local(sizes, adjoint, saved_state, wind_field, facade_slot, facade_table, impedance):
    imp = impedance.reshape(-1, 128)
    hbm_spec = pl.BlockSpec(memory_space=pltpu.HBM)
    vmem_spec = pl.BlockSpec(memory_space=pltpu.VMEM)
    v = pltpu.VMEM
    dma = pltpu.SemaphoreType.DMA
    steps = saved_state.shape[0]
    assert steps == 4
    state, sums = pl.pallas_call(
        functools.partial(kernel, sizes),
        out_shape=[
            jax.ShapeDtypeStruct(adjoint.shape, F32),
            jax.ShapeDtypeStruct((FAC_DEV,), F32),
        ],
        in_specs=[hbm_spec] * 6,
        out_specs=[vmem_spec, vmem_spec],
        scratch_shapes=[
            v((4, 8, 8, 128), F32),
            v((4, 8, 8, 128), F32),
            v((steps, 4, 8, 8, 128), F32),
            v((3, 8, 8, 128), F32),
            v((8, 8, 128), jnp.int32),
            v((1, 64), jnp.int32),
            v((128, 128), F32),
            v((FIELDS * 10 * 4, 8, 128), F32),
            v((32, 8, 128), F32),
            v((8, 8, 128), F32),
            v((2, 24, 8, 128), F32),
            v((2, 24, 128), F32),
            v((2, 3, 8, 128), F32),
            v((2, 2, 8, 128), F32),
            v((17, 8, 128), F32),
            v((2, 24, 8, 128), F32),
            v((2, 24, 128), F32),
            v((2, 3, 8, 128), F32),
            v((2, 8, 128), F32),
            v((17, 8, 128), F32),
            v((2, 2, 8, 128), F32),
            v((2, 2, 8, 128), F32),
            v((2, 32, 128), F32),
            v((2, 8, 128), F32),
            v((4, 8, 128), F32),
            v((2, 32, 128), F32),
            v((2, 8, 128), F32),
            v((4, 8, 128), F32),
            v((64, 8, 128), F32),
            v((64, 128), F32),
            v((8, 128), F32),
            v((2, 8, 128), F32),
            dma((7,)), dma((17,)), dma((17,)), dma((5,)), dma((5,)), dma((2,)), dma((2,)),
        ],
        compiler_params=pltpu.CompilerParams(
            collective_id=0, has_side_effects=True, vmem_limit_bytes=32 << 20
        ),
    )(*[pltpu.with_memory_space_constraint(a, pltpu.HBM)
        for a in (adjoint, saved_state, wind_field, facade_slot, facade_table, imp)])
    out, grad = pl.pallas_call(
        writer,
        out_shape=[
            jax.ShapeDtypeStruct(adjoint.shape, F32),
            jax.ShapeDtypeStruct((FAC_DEV,), F32),
        ],
        in_specs=[vmem_spec, vmem_spec],
        out_specs=[hbm_spec, hbm_spec],
        scratch_shapes=[dma((3,))],
        compiler_params=pltpu.CompilerParams(vmem_limit_bytes=1 << 20),
    )(state, sums)
    return out, grad


def solution(mesh):
    sizes = tuple(mesh.shape[a] for a in ("gx", "gy", "gz"))
    return jax.shard_map(
        functools.partial(local, sizes),
        mesh=mesh,
        in_specs=(
            P(None, None, "gz", "gx", "gy"),
            P(None, None, "gz", "gx", "gy"),
            P(None, "gz", "gx", "gy"),
            P("gz", "gx", "gy"),
            P("gz", "gx", "gy", None),
            P(),
        ),
        out_specs=(P(None, None, "gz", "gx", "gy"), P(("gx", "gy", "gz"))),
        check_vma=False,
    )
```

```python
import functools

import jax
import jax.numpy as jnp
from jax import lax
from jax.experimental import pallas as pl
from jax.experimental.pallas import tpu as pltpu
from jax.sharding import PartitionSpec as P

FAC_DEV = 32
TIME_STEP = 0.3
HALF = TIME_STEP
FULL = 2.0 * TIME_STEP
MESH = pl.DeviceIdType.MESH
F32 = jnp.float32

WIND, DAMP, FIELDS = 8, 11, 12
OWN, XH, YH, XYH = 0, 1, 2, 3


def when(cond, run):
    if cond is None:
        run()
    else:
        pl.when(cond)(run)


class Sent:
    def __init__(self, src, dst, send_sem, recv_sem, to, send_if=None, recv_if=None):
        self.copy = pltpu.make_async_remote_copy(
            src_ref=src, dst_ref=dst, send_sem=send_sem, recv_sem=recv_sem, device_id=to, device_id_type=MESH
        )
        self.send_if, self.recv_if = send_if, recv_if

    def start(self):
        when(self.send_if, self.copy.start)

    def wait_recv(self):
        when(self.recv_if, self.copy.wait_recv)

    def wait_send(self):
        when(self.send_if, self.copy.wait_send)


def kernel(sizes, adj, saved, wind, slot, table, impedance, out, grad,
           mid, upp, sav, win, slo, tab, imp, ext, part, prod,
           xbuf, xzbuf, ybuf, xybuf, zbuf, xr, xzr, yr, yzr, zr, xyr, xyzr,
           xs, ys, zs, xf, yf, zf, slots, smat, gs, gr,
           in_sem, ss, rs, fs, fr, g_ss, g_rs):
    nx, ny, nz = sizes
    ix, iy, iz = lax.axis_index("gx"), lax.axis_index("gy"), lax.axis_index("gz")
    has_right, has_left = ix < nx - 1, ix > 0

    def device(dx, dy, dz):
        return (
            lax.rem(ix + dx + nx, nx) if dx else ix,
            lax.rem(iy + dy + ny, ny) if dy else iy,
            1 - iz if dz else iz,
        )

    barrier = pltpu.get_barrier_semaphore()
    for dx in (0, 1, -1):
        def greet(dx=dx):
            for dy in (0, 1, -1):
                for dz in (1, 0):
                    if dx or dy or dz:
                        pl.semaphore_signal(barrier, inc=1, device_id=device(dx, dy, dz), device_id_type=MESH)

        when({0: None, 1: has_right, -1: has_left}[dx], greet)

    loads = []
    for i, (src, dst) in enumerate(
        [(table.at[0, 0], tab), (impedance, imp), (slot, slo), (wind, win), (adj.at[1], mid), (adj.at[0], upp), (saved, sav)]
    ):
        copy = pltpu.make_async_copy(src, dst, in_sem.at[i])
        copy.start()
        loads.append(copy)

    lane = lax.broadcasted_iota(jnp.int32, (8, 128), 1)
    row = lax.broadcasted_iota(jnp.int32, (8, 128), 0)
    row0, row7, lane0, lane127 = row == 0, row == 7, lane == 0, lane == 127
    quarter = jnp.bitwise_and(lane, 3)
    x_in = ((row < 4) & has_right) | ((row >= 4) & has_left)
    y_in = ((lane < 64) & (iy < ny - 1)) | ((lane >= 64) & (iy > 0))
    inside = {OWN: None, XH: x_in, YH: y_in, XYH: x_in & y_in}
    flipped = iz == 1
    hz = jnp.where(flipped, -HALF, HALF)

    def plane(z):
        return jnp.where(flipped, 7 - z, z)

    def put(f, z, t, value):
        ext[(f * 10 + z) * 4 + t] = value

    def get(f, z, t):
        return ext[(f * 10 + z) * 4 + t]

    for i in range(3):
        loads[i].wait()
    group = iy * nz + iz
    per_row = 128 // FAC_DEV
    stride = (ny * nz) // per_row
    row_of = [lax.rem(ix + o + nx, nx) * stride + group // per_row for o in (0, 1, -1)]
    ids = jnp.broadcast_to(jnp.concatenate([tab[...], tab[...]], axis=1), (8, 128))
    id_row = lax.shift_right_logical(ids, 7)
    id_lane = jnp.bitwise_and(ids, 127)
    lut = jnp.zeros((8, 128), F32)
    for o in range(3):
        line = jnp.broadcast_to(imp[pl.ds(row_of[o], 1), :], (8, 128))
        lut = jnp.where(id_row == row_of[o], jnp.take_along_axis(line, id_lane, axis=1), lut)
    lut = lut * FULL
    place = jnp.where(id_row == row_of[0], 0, jnp.where(id_row == row_of[1], 32, 64)) + jnp.bitwise_and(ids, 31)
    for z in range(8):
        names = slo[plane(z)]
        value = jnp.take_along_axis(lut, jnp.maximum(names - 1, 0), axis=1)
        put(DAMP, z, OWN, jnp.where(names > 0, value, 0.0))
    for i in range(3, 6):
        loads[i].wait()

    def fluxes(s, w):
        fz = [w[0] * v for v in s]
        fx = [w[1] * v for v in s]
        fy = [w[2] * v for v in s]
        fz[0], fz[1] = fz[0] + s[1], fz[1] + s[0]
        fx[0], fx[2] = fx[0] + s[2], fx[2] + s[0]
        fy[0], fy[3] = fy[0] + s[3], fy[3] + s[0]
        return fz, fx, fy

    zero = jnp.zeros((8, 128), F32)

    def within(level, allf, upper, store):
        for z in range(8):
            d = get(DAMP, z, OWN)
            for c in range(4):
                fz, fx, fy = (allf[z][i][c] for i in range(3))
                dx = jnp.where(row7, 0.0, pltpu.roll(fx, 7, 0)) - jnp.where(row0, 0.0, pltpu.roll(fx, 1, 0))
                dy = jnp.where(lane127, 0.0, pltpu.roll(fy, 127, 1)) - jnp.where(lane0, 0.0, pltpu.roll(fy, 1, 1))
                value = upper(c, z) + HALF * (dx + dy) - d * level(c, z)
                if 0 < z < 7:
                    value = value + hz * (allf[z + 1][0][c] - allf[z - 1][0][c])
                elif z == 0:
                    value = value + hz * allf[1][0][c]
                else:
                    value = value - hz * allf[6][0][c]
                store(c, z, value)

    allf = []
    for z in range(8):
        zi = plane(z)
        own = [mid[c, zi] for c in range(4)]
        wz = [win[c, zi] for c in range(3)]
        for c in range(4):
            put(c, z, OWN, own[c])
        for c in range(3):
            put(WIND + c, z, OWN, wz[c])
        allf.append(fluxes(own, wz))
    within(
        lambda c, z: get(c, z, OWN), allf, lambda c, z: upp[c, plane(z)], lambda c, z, value: put(4 + c, z, OWN, value)
    )

    y_high, y_low = [zero] * 3, [zero] * 3
    for z in reversed(range(8)):
        for f in range(FIELDS):
            value = get(f, z, OWN)
            if z == 7:
                zbuf[f] = value
            if z == 6 and 4 <= f <= WIND:
                zbuf[FIELDS + f - 4] = value
            n = (7 - z) * FIELDS + f
            k = n % 4
            if k == 0:
                x_high = x_low = zero
            moved = pltpu.roll(value, (2 * k + 2) % 8, 0)
            pair, k_next = row // 2, (k + 1) % 4
            x_high = jnp.where(pair == k, moved, x_high)
            x_low = jnp.where(pair == k_next, moved, x_low)
            if k == 3:
                xbuf[0, n // 4] = x_high
                xbuf[1, n // 4] = x_low
            t, k = n // 32, n % 32
            moved = pltpu.roll(value, (4 * k + 2) % 128, 1)
            quad = lane // 4 == k
            y_high[t] = jnp.where(quad & (quarter < 2), moved, y_high[t])
            y_low[t] = jnp.where(quad & (quarter >= 2), moved, y_low[t])
            if z == 7 and f < WIND + 2:
                xzbuf[0, pl.ds(f, 1), :] = value[7:8]
                xzbuf[1, pl.ds(f, 1), :] = value[0:1]
    for c in range(4):
        xzbuf[0, pl.ds(10 + c, 1), :] = allf[7][0][c][6:7]
        xzbuf[1, pl.ds(10 + c, 1), :] = allf[7][0][c][1:2]
        xzbuf[0, pl.ds(14 + c, 1), :] = allf[6][1][c][7:8]
        xzbuf[1, pl.ds(14 + c, 1), :] = allf[6][1][c][0:1]
    for side, tiles in ((0, y_high), (1, y_low)):
        xy_high, xy_low = zero, zero
        for t in range(3):
            ybuf[side, t] = tiles[t]
            moved = pltpu.roll(tiles[t], (2 * t + 2) % 8, 0)
            xy_high = jnp.where(row // 2 == t, moved, xy_high)
            xy_low = jnp.where(row // 2 == t + 1, moved, xy_low)
        xybuf[0, side] = xy_high
        xybuf[1, side] = xy_low

    halo = {}

    def post(kind, src, dst, to, dx=0):
        i = sum(len(group) for group in halo.values())
        send_if, recv_if = {0: (None, None), 1: (has_right, has_left), -1: (has_left, has_right)}[dx]
        halo.setdefault(kind, []).append(Sent(src, dst, ss.at[i], rs.at[i], to, send_if, recv_if))

    both = ((0, 1), (1, -1))
    for side, d in both:
        for x_side, e in both:
            post("xy", xybuf.at[x_side, side], xyr.at[x_side, side], device(e, d, 0), e)
        post("y", ybuf.at[side], yr.at[side], device(0, d, 0))
        post("x", xbuf.at[side], xr.at[side], device(d, 0, 0), d)
    post("z", zbuf, zr, device(0, 0, 1))
    for side, d in both:
        post("xz", xzbuf.at[side], xzr.at[side], device(d, 0, 1), d)
        post("yz", ybuf.at[side, 0], yzr.at[side], device(0, d, 1))
        for x_side, e in both:
            post("xyz", xybuf.at[x_side, side], xyzr.at[x_side, side], device(e, d, 1), e)

    @pl.when(has_left & has_right)
    def _():
        pl.semaphore_wait(barrier, 17)

    @pl.when(ix == 0)
    def _():
        pl.semaphore_wait(barrier, 11)
        pl.semaphore_signal(barrier, inc=1, device_id=(nx - 1, iy, iz), device_id_type=MESH)

    @pl.when(ix == nx - 1)
    def _():
        pl.semaphore_wait(barrier, 12)
        pl.semaphore_signal(barrier, inc=1, device_id=(0, iy, iz), device_id_type=MESH)

    odd = lax.rem(ix, 2) == 1

    def start(*kinds):
        for kind in kinds:
            for sent in halo[kind]:
                sent.start()

    pl.when(odd)(lambda: start("y", "yz", "z", "x", "xy", "xz", "xyz"))
    pl.when(jnp.logical_not(odd))(lambda: start("x", "xy", "xz", "xyz", "y", "yz", "z"))

    def arrived(*kinds):
        for kind in kinds:
            for sent in halo[kind]:
                sent.wait_recv()

    def add_products(k, base, planes):
        for z in planes:
            zi = plane(z)
            total = get(base, z, OWN) * sav[k, 0, zi]
            for c in range(1, 4):
                total = total + get(base + c, z, OWN) * sav[k, c, zi]
            prod[z] = total if k == 0 else prod[z] + total

    loads[6].wait()
    add_products(0, 0, range(8))

    def masked(f, t, value):
        if f < 4 or WIND <= f < DAMP:
            return jnp.where(inside[t], value, 0.0)
        return value

    def both_y(high, low):
        return jnp.where(quarter < 2, high, low)

    def xy_tile(src, t):
        value = jnp.where(row // 2 == t, both_y(src[0, 0], src[0, 1]), both_y(src[1, 0], src[1, 1]))
        return pltpu.roll(value, (6 - 2 * t) % 8, 0)

    def each(run):
        for z in range(8):
            for f in range(FIELDS):
                run(z, f, (7 - z) * FIELDS + f)

    def unpack_x(z, f, n):
        k = n % 4
        value = jnp.where(row // 2 == k, xr[0, n // 4], xr[1, n // 4])
        put(f, z, XH, masked(f, XH, pltpu.roll(value, (6 - 2 * k) % 8, 0)))

    def unpack_y(z, f, n):
        put(f, z, YH, masked(f, YH, pltpu.roll(y_own[n // 32], (126 - 4 * (n % 32)) % 128, 1)))

    def unpack_xy(z, f, n):
        if f < DAMP:
            put(f, z, XYH, masked(f, XYH, pltpu.roll(xy_own[n // 32], (126 - 4 * (n % 32)) % 128, 1)))

    def unpack_top():
        y_top = both_y(yzr[0], yzr[1])
        xy_top = xy_tile(xyzr, 0)
        for f in range(FIELDS):
            put(f, 8, OWN, zr[f])
            if 4 <= f <= WIND:
                put(f, 9, OWN, zr[FIELDS + f - 4])
            if f < WIND + 2:
                value = jnp.where(row == 7, xzr[0, pl.ds(f, 1), :], xzr[1, pl.ds(f, 1), :])
                put(f, 8, XH, masked(f, XH, value))
            shift = (126 - 4 * f) % 128
            if f < DAMP:
                put(f, 8, YH, masked(f, YH, pltpu.roll(y_top, shift, 1)))
            if f < 4 or WIND <= f < DAMP:
                put(f, 8, XYH, masked(f, XYH, pltpu.roll(xy_top, shift, 1)))
                put(f, 9, YH, masked(f, YH, pltpu.roll(y_top, (126 - 4 * (FIELDS + f)) % 128, 1)))

    def across(own, far, r_up, r_dn, axis):
        size = own.shape[axis]
        up, dn = size - 1, 1
        own_up, own_dn = pltpu.roll(own, up, axis), pltpu.roll(own, dn, axis)
        far_up, far_dn = pltpu.roll(far, up, axis), pltpu.roll(far, dn, axis)
        return (
            jnp.where(r_up, far_up, own_up) - jnp.where(r_dn, far_dn, own_dn),
            jnp.where(r_up, own_up, far_up) - jnp.where(r_dn, own_dn, far_dn),
        )

    def flux_tile(src, z, t):
        return fluxes([get(src + c, z, t) for c in range(4)], [get(WIND + c, z, t) for c in range(3)])

    def flux_plane(src, z, tiles):
        return {t: flux_tile(src, z, t) for t in tiles}

    def seam(flux, r_up, r_dn, axis):
        size = flux.shape[axis]
        return jnp.where(r_up, pltpu.roll(flux, size - 1, axis), 0.0) - jnp.where(r_dn, pltpu.roll(flux, 1, axis), 0.0)

    every, sides = [OWN, XH, YH, XYH], [OWN, XH, YH]
    beside_x = {OWN: XH, XH: OWN, YH: XYH, XYH: YH}
    beside_y = {OWN: YH, YH: OWN, XH: XYH, XYH: XH}

    def first_plane(z):
        if z < 8:
            return flux_plane(0, z, every)
        if z == 8:
            result = flux_plane(0, 8, every)
            fz = result[XH][0]
            for c in range(4):
                lo, hi = xzr[0, pl.ds(10 + c, 1), :], xzr[1, pl.ds(10 + c, 1), :]
                fz[c] = jnp.where(row == 6, lo, jnp.where(row == 1, hi, fz[c]))
            return result
        fx = []
        for c in range(4):
            lo, hi = xzr[0, pl.ds(14 + c, 1), :], xzr[1, pl.ds(14 + c, 1), :]
            fx.append(jnp.where(inside[XH], jnp.where(row == 7, lo, hi), 0.0))
        return {XH: (None, fx, None), YH: flux_tile(0, 9, YH)}

    def first_step(planes):
        held = {}
        for z in planes:
            for w in ([z - 1, z] if z == 8 else [z, z + 1] if z == 7 else [z]):
                if w not in held:
                    held[w] = first_plane(w)
            here = held[z]
            for t in every if z < 8 else sides if z == 8 else [OWN]:
                for c in range(4):
                    sx = seam(here[beside_x[t]][1][c], row7, row0, 0)
                    sy = seam(here[beside_y[t]][2][c], lane127, lane0, 1)
                    value = get(4 + c, z, t) + HALF * (sx + sy)
                    if z == 7:
                        value = value + hz * held[8][t][0][c]
                    if z == 8:
                        value = value - hz * held[7][t][0][c]
                    if t != OWN:
                        value = jnp.where(inside[t], value, 0.0)
                    put(4 + c, z, t, value)

    def step(src, dst, planes, flux_tiles, new_tiles, keep=None):
        held = {}
        for z in planes:
            for w in (z - 1, z, z + 1):
                if w >= 0 and w not in held:
                    held[w] = flux_plane(src, w, flux_tiles[w])
            f = held[z]
            for c in range(4):
                dx, dy = {}, {}
                dx[OWN], dx[XH] = across(f[OWN][1][c], f[XH][1][c], row7, row0, 0)
                dy[OWN], dy[YH] = across(f[OWN][2][c], f[YH][2][c], lane127, lane0, 1)
                if XYH in f:
                    dx[YH], dx[XYH] = across(f[YH][1][c], f[XYH][1][c], row7, row0, 0)
                    dy[XH], dy[XYH] = across(f[XH][2][c], f[XYH][2][c], lane127, lane0, 1)
                for t in new_tiles[z]:
                    dz = held[z + 1][t][0][c]
                    if z > 0:
                        dz = dz - held[z - 1][t][0][c]
                    value = get(dst + c, z, t) + HALF * (dx[t] + dy[t]) + hz * dz - get(DAMP, z, t) * get(src + c, z, t)
                    if t != OWN:
                        value = jnp.where(inside[t], value, 0.0)
                    put(dst + c, z, t, value)
                    if keep is not None:
                        keep(c, z, value)

    def second_step(planes):
        step(4, 0, planes, [every] * 8 + [sides, [OWN]], [sides] * 8 + [[OWN]])

    def keep(c, z, value):
        out[0, c, plane(z)] = value

    def third_step(planes):
        step(0, 4, planes, [sides] * 8 + [[OWN]], [[OWN]] * 8, keep)

    arrived("x")
    each(unpack_x)
    arrived("y")
    y_own = [both_y(yr[0, t], yr[1, t]) for t in range(3)]
    each(unpack_y)
    arrived("xy")
    xy_own = [xy_tile(xyr, t) for t in range(3)]
    each(unpack_xy)
    first_step(range(7))
    add_products(1, 4, range(7))
    second_step(range(6))
    add_products(2, 0, range(6))
    third_step(range(5))
    add_products(3, 4, range(5))

    def slot_sum(s, planes):
        total = zero
        for z in planes:
            total = total + jnp.where(slo[plane(z)] == s + 1, prod[z], 0.0)
        return total

    for s in range(64):
        slots[s] = slot_sum(s, range(5))
    turned = jnp.transpose(jnp.broadcast_to(place[0:1], (128, 128)))[0:64]
    wide = lax.broadcasted_iota(jnp.int32, (64, 128), 1)
    arrived("z", "yz", "xz", "xyz")
    unpack_top()
    first_step(range(7, 10))
    add_products(1, 4, [7])
    second_step(range(6, 9))
    add_products(2, 0, [6, 7])
    third_step(range(5, 8))
    add_products(3, 4, [5, 6, 7])

    for s in range(64):
        total = slots[s] + slot_sum(s, range(5, 8))
        smat[pl.ds(s, 1), :] = jnp.sum(total, axis=0, keepdims=True)
    sums = jnp.sum(smat[...], axis=1, keepdims=True) * (-FULL)
    facades = jnp.sum(jnp.where(turned == wide, sums, 0.0), axis=0, keepdims=True)
    gs[...] = jnp.broadcast_to(facades, (8, 128))

    @pl.when(ix == 0)
    def _():
        pl.semaphore_wait(barrier, 1)

    parts = [
        Sent(gs, gr.at[0], g_ss.at[0], g_rs.at[0], device(1, 0, 0)),
        Sent(gs, gr.at[1], g_ss.at[1], g_rs.at[1], device(-1, 0, 0)),
    ]
    for sent in parts:
        sent.start()

    low, high = zero, zero
    allf = []
    for z in range(8):
        fz, fx, fy = fluxes([get(4 + c, z, OWN) for c in range(4)], [get(WIND + c, z, OWN) for c in range(3)])
        allf.append((fz, fx, fy))
        for c in range(4):
            n = c * 8 + z
            xs[0, pl.ds(n, 1), :] = fx[c][7:8]
            xs[1, pl.ds(n, 1), :] = fx[c][0:1]
            p = 2 * n + 1
            moved = pltpu.roll(fy[c], (p + 1) % 128, 1)
            high = jnp.where(lane == p, moved, high)
            low = jnp.where(lane == (p + 1) % 128, moved, low)
    ys[0], ys[1] = high, low
    for c in range(4):
        zs[c] = allf[7][0][c]
    faces = [
        Sent(ys.at[0], yf.at[0], fs.at[0], fr.at[0], device(0, 1, 0)),
        Sent(ys.at[1], yf.at[1], fs.at[1], fr.at[1], device(0, -1, 0)),
        Sent(zs, zf, fs.at[2], fr.at[2], device(0, 0, 1)),
        Sent(xs.at[0], xf.at[0], fs.at[3], fr.at[3], device(1, 0, 0), has_right, has_left),
        Sent(xs.at[1], xf.at[1], fs.at[4], fr.at[4], device(-1, 0, 0), has_left, has_right),
    ]
    for sent in faces:
        sent.start()
    def hold(c, z, value):
        part[c * 8 + z] = value

    within(lambda c, z: get(4 + c, z, OWN), allf, lambda c, z: get(c, z, OWN), hold)

    for sent in faces:
        sent.wait_recv()
    south = jnp.where(iy > 0, -yf[0], 0.0)
    north = jnp.where(iy < ny - 1, pltpu.roll(yf[1], 126, 1), 0.0)
    rim = HALF * jnp.where(jnp.bitwise_and(lane, 1) == 1, south, north)
    at_left, at_right = row0 & has_left, row7 & has_right
    for z in range(8):
        for c in range(4):
            n = c * 8 + z
            value = part[n]
            edge = pltpu.roll(rim, 128 - (2 * n + 1), 1)
            value = value + jnp.where(lane0 | lane127, edge, 0.0)
            lrow = xf[0, pl.ds(n, 1), :] * (-HALF)
            rrow = xf[1, pl.ds(n, 1), :] * HALF
            value = value + jnp.where(at_left, lrow, jnp.where(at_right, rrow, 0.0))
            if z == 7:
                value = value + hz * zf[c]
            out[1, c, plane(z)] = value
    for sent in sum(halo.values(), []) + faces + parts:
        sent.wait_send()
    for sent in parts:
        sent.wait_recv()
    total = gs[...] + pltpu.roll(gr[0], 96, 1) + pltpu.roll(gr[1], 64, 1)
    grad[...] = total[0, 0:FAC_DEV]


def writer(state, sums, out, grad, sems):
    copies = [pltpu.make_async_copy(sums, grad, sems.at[0])]
    for level in range(2):
        copies.append(pltpu.make_async_copy(state.at[level], out.at[level], sems.at[1 + level]))
    for copy in copies:
        copy.start()
    for copy in copies:
        copy.wait()


def local(sizes, adjoint, saved_state, wind_field, facade_slot, facade_table, impedance):
    imp = impedance.reshape(-1, 128)
    hbm_spec = pl.BlockSpec(memory_space=pltpu.HBM)
    vmem_spec = pl.BlockSpec(memory_space=pltpu.VMEM)
    v = pltpu.VMEM
    dma = pltpu.SemaphoreType.DMA
    steps = saved_state.shape[0]
    assert steps == 4
    state, sums = pl.pallas_call(
        functools.partial(kernel, sizes),
        out_shape=[
            jax.ShapeDtypeStruct(adjoint.shape, F32),
            jax.ShapeDtypeStruct((FAC_DEV,), F32),
        ],
        in_specs=[hbm_spec] * 6,
        out_specs=[vmem_spec, vmem_spec],
        scratch_shapes=[
            v((4, 8, 8, 128), F32),
            v((4, 8, 8, 128), F32),
            v((steps, 4, 8, 8, 128), F32),
            v((3, 8, 8, 128), F32),
            v((8, 8, 128), jnp.int32),
            v((1, 64), jnp.int32),
            v((128, 128), F32),
            v((FIELDS * 10 * 4, 8, 128), F32),
            v((32, 8, 128), F32),
            v((8, 8, 128), F32),
            v((2, 24, 8, 128), F32),
            v((2, 24, 128), F32),
            v((2, 3, 8, 128), F32),
            v((2, 2, 8, 128), F32),
            v((17, 8, 128), F32),
            v((2, 24, 8, 128), F32),
            v((2, 24, 128), F32),
            v((2, 3, 8, 128), F32),
            v((2, 8, 128), F32),
            v((17, 8, 128), F32),
            v((2, 2, 8, 128), F32),
            v((2, 2, 8, 128), F32),
            v((2, 32, 128), F32),
            v((2, 8, 128), F32),
            v((4, 8, 128), F32),
            v((2, 32, 128), F32),
            v((2, 8, 128), F32),
            v((4, 8, 128), F32),
            v((64, 8, 128), F32),
            v((64, 128), F32),
            v((8, 128), F32),
            v((2, 8, 128), F32),
            dma((7,)), dma((17,)), dma((17,)), dma((5,)), dma((5,)), dma((2,)), dma((2,)),
        ],
        compiler_params=pltpu.CompilerParams(
            collective_id=0, has_side_effects=True, vmem_limit_bytes=32 << 20
        ),
    )(*[pltpu.with_memory_space_constraint(a, pltpu.HBM)
        for a in (adjoint, saved_state, wind_field, facade_slot, facade_table, imp)])
    out, grad = pl.pallas_call(
        writer,
        out_shape=[
            jax.ShapeDtypeStruct(adjoint.shape, F32),
            jax.ShapeDtypeStruct((FAC_DEV,), F32),
        ],
        in_specs=[vmem_spec, vmem_spec],
        out_specs=[hbm_spec, hbm_spec],
        scratch_shapes=[dma((3,))],
        compiler_params=pltpu.CompilerParams(vmem_limit_bytes=1 << 20),
    )(state, sums)
    return out, grad


def solution(mesh):
    sizes = tuple(mesh.shape[a] for a in ("gx", "gy", "gz"))
    return jax.shard_map(
        functools.partial(local, sizes),
        mesh=mesh,
        in_specs=(
            P(None, None, "gz", "gx", "gy"),
            P(None, None, "gz", "gx", "gy"),
            P(None, "gz", "gx", "gy"),
            P("gz", "gx", "gy"),
            P("gz", "gx", "gy", None),
            P(),
        ),
        out_specs=(P(None, None, "gz", "gx", "gy"), P(("gx", "gy", "gz"))),
        check_vma=False,
    )
```
